32 devices in a mesh: seq: 8 (over z, y), head: 4 (over x, core).
Axes of the slice: x: 2, y: 2, z: 4, core: 2. Of those that a mesh axis runs over, the one named last changes fastest.
Arguments:
- tokens: bfloat16 [2048, 3072], P('seq'), may hold values from -18 to 18
- w_qkv: bfloat16 [3, 3072, 2048], P(None, 'seq', 'head'), may hold values from -0.109375 to 0.109375
- gains: float32 [2, 2048], P(None, 'head'), may hold values from 0.5 to 1.5
- cotangent: bfloat16 [2048, 2048], P('seq', 'head'), may hold values from -6 to 6
- token_clip: int32 [2048], replicated, may hold values from 0 to 2, as said below
- key_live: int32 [2048], replicated, may hold values 0 or 1
- damp_mask: int32 [3072, 2048], P('seq', 'head'), may hold values 0 or 1
Outputs:
- fisher_ratio: float32 [3, 3072, 2048], P(None, 'seq', 'head')
- dampened: bfloat16 [3, 3072, 2048], P(None, 'seq', 'head')
The draws below stay inside these ranges and needn't reach their ends.
Inputs may be any that keep to these rules, and one draw needn't show every extreme that they name: token_clip never decreases along the tokens (each clip is one contiguous run of tokens); every clip has at least one token and the longest has exactly 1536.
All inputs are finite; a program needn't handle non-finite values. No bound on the sum of `damp_mask` on one device may be relied on, other than what follows from the above.
Results may differ from the reference program's by a relative error of at most 0.03.
Values may be sent and summed in bfloat16 or wider, within the bound.
No kernel may reach another device: no remote copies, remote signals or barrier semaphores. Data moves between devices by JAX's collectives and lax.ppermute only.
A program may use at most 192 MiB of HBM per device.

```python
import math
import jax
import jax.numpy as jnp
from jax import lax

D = 3072
HD = 128
HEADS = 16
CLIPS = 3
TOK_DEV = 256
TOKENS = 2048
HID = 2048
N_SEQ = 8


def draw_tokens(key, part):
    column = jnp.arange(D, dtype=jnp.float32) / float(D - 1)
    base = jnp.clip(jax.random.normal(key, (TOKENS, D), jnp.float32), -6.0, 6.0)
    low_scale = 0.5
    high_scale = 2.0
    scales = low_scale * jnp.exp(column * jnp.log(high_scale / low_scale))
    return (base * scales[None, :]).astype(jnp.bfloat16)


def draw_token_clip(key, part):
    longest = 3 * TOKENS // 4
    remain = TOKENS - longest
    key_split = jax.random.fold_in(key, 11)
    key_place = jax.random.fold_in(key, 23)
    first_rest = jax.random.randint(key_split, (), 1, remain, dtype=jnp.int32)
    second_rest = remain - first_rest
    place = jax.random.randint(key_place, (), 0, 3, dtype=jnp.int32)
    length_zero = jnp.where(place == 0, longest, first_rest)
    length_one = jnp.where(place == 1, longest, jnp.where(place == 0, first_rest, second_rest))
    bound_one = length_zero
    bound_two = length_zero + length_one
    positions = jnp.arange(TOKENS, dtype=jnp.int32)
    return (positions >= bound_one).astype(jnp.int32) + (positions >= bound_two).astype(jnp.int32)


def touch_ends(array, key, smallest, high):
    index_at = [jax.random.randint(jax.random.fold_in(key, axis), (), 0, length) for axis, length in enumerate(array.shape)]
    widest = array.shape.index(max(array.shape))
    neighbour = index_at[:widest] + [(index_at[widest] + 1) % array.shape[widest]] + index_at[widest + 1:]
    return array.at[tuple(index_at)].set(smallest).at[tuple(neighbour)].set(high)


def block_levels(stream_key, dims, split, low, top_value):
    loudness = 1.0
    for dim, blocks in split:
        steps = jax.random.uniform(jax.random.fold_in(jax.random.fold_in(stream_key, 6), dim), (blocks,), jnp.float32, low / len(split), top_value / len(split))
        loudness = loudness * jnp.repeat(jnp.exp(steps), dims[dim] // blocks).reshape((-1,) + (1,) * (len(dims) - 1 - dim))
    return loudness


def scatter_about(rng, shape, spread, reach, pieces=(), kind=jnp.bfloat16):
    drawn = spread * jax.random.normal(rng, shape, jnp.float32)
    if pieces:
        drawn = drawn * block_levels(rng, shape, pieces, -0.22, 0.18)
    return jnp.clip(drawn, -reach, reach).astype(kind)


def setup_inputs(seed: int = 0) -> dict:
    key_list = jax.random.split(jax.random.key(seed), 8)
    return {
        "tokens": draw_tokens(jax.random.fold_in(key_list[7], 71), 0),
        "w_qkv": scatter_about(key_list[1], (3, D, HID), D ** -0.5, 0.109375, ((1, 8), (2, 4))),
        "gains": jnp.clip(1.0 + 0.1 * jax.random.normal(key_list[2], (2, HID), jnp.float32), 0.5, 1.5),
        "cotangent": scatter_about(key_list[3], (TOKENS, HID), 1.0, 6.0, ((0, 8), (1, 4))),
        "token_clip": draw_token_clip(jax.random.fold_in(key_list[7], 71), 0),
        "key_live": touch_ends((jax.random.randint(key_list[5], (TOKENS,), 0, 4) < 3).astype(jnp.int32), jax.random.fold_in(key_list[5], 1), 0, 1),
        "damp_mask": touch_ends((jax.random.randint(key_list[6], (D, HID), 0, 2) < 1).astype(jnp.int32), jax.random.fold_in(key_list[6], 1), 0, 1),
    }


def normed(values, gain_row):
    shaped = values.reshape(TOKENS, HEADS, HD)
    inverse = lax.rsqrt(lax.optimization_barrier(jnp.mean(shaped * shaped, -1, keepdims=True)) + 1e-06)
    return (shaped * inverse * gain_row.reshape(HEADS, HD), inverse, shaped)

def unnorm(upstream, shaped, inverse, gain_row):
    gain_grid = gain_row.reshape(HEADS, HD)
    cubed = inverse * inverse * inverse
    return inverse * gain_grid * upstream - shaped * cubed * lax.optimization_barrier(jnp.mean(shaped * gain_grid * upstream, -1, keepdims=True))

def reference(tokens, w_qkv, gains, cotangent, token_clip, key_live, damp_mask):
    score_scale = 1.0 / math.sqrt(HD)
    projected = [jnp.dot(tokens, w_qkv[index], preferred_element_type=jnp.float32) for index in range(3)]
    query_n, query_inv, query_raw = normed(projected[0], gains[0])
    key_n, key_inv, key_raw = normed(projected[1], gains[1])
    query_b = jnp.transpose(query_n.astype(jnp.bfloat16), (1, 0, 2))
    key_b = jnp.transpose(key_n.astype(jnp.bfloat16), (1, 0, 2))
    value_b = jnp.transpose(projected[2].astype(jnp.bfloat16).reshape(TOKENS, HEADS, HD), (1, 0, 2))
    grad_out = jnp.transpose(cotangent.reshape(TOKENS, HEADS, HD), (1, 0, 2))
    positions = jnp.arange(TOKENS, dtype=jnp.int32)
    allowed = (token_clip[:, None] == token_clip[None, :]) & ((key_live[None, :] == 1) | (positions[:, None] == positions[None, :]))

    def per_head(operands):
        head_q, head_k, head_v, head_o = operands
        scores = jnp.dot(head_q, head_k.T, preferred_element_type=jnp.float32) * score_scale
        scores = jnp.where(allowed, scores, -1e+30)
        peak = lax.optimization_barrier(jnp.max(scores, -1, keepdims=True))
        expd = jnp.exp(scores - peak)
        probs = expd / lax.optimization_barrier(jnp.sum(expd, -1, keepdims=True))
        grad_p = jnp.dot(head_o, head_v.T, preferred_element_type=jnp.float32)
        row_dot = lax.optimization_barrier(jnp.sum(probs * grad_p, -1, keepdims=True))
        ds_half = (probs * (grad_p - row_dot)).astype(jnp.bfloat16)
        probs_half = probs.astype(jnp.bfloat16)
        grad_qn = jnp.dot(ds_half, head_k, preferred_element_type=jnp.float32) * score_scale
        ds_groups = ds_half.reshape(N_SEQ, TOK_DEV, TOKENS).astype(jnp.float32)
        pr_groups = probs_half.reshape(N_SEQ, TOK_DEV, TOKENS).astype(jnp.float32)
        q_groups = head_q.reshape(N_SEQ, TOK_DEV, HD).astype(jnp.float32)
        o_groups = head_o.reshape(N_SEQ, TOK_DEV, HD).astype(jnp.float32)
        key_parts = jnp.einsum('nik,nic->nkc', ds_groups, q_groups) * score_scale
        value_parts = jnp.einsum('nik,nic->nkc', pr_groups, o_groups)
        key_sum = lax.optimization_barrier(jnp.sum(lax.optimization_barrier(key_parts.astype(jnp.bfloat16)).astype(jnp.float32), 0))
        value_sum = lax.optimization_barrier(jnp.sum(lax.optimization_barrier(value_parts.astype(jnp.bfloat16)).astype(jnp.float32), 0))
        return (grad_qn, key_sum, value_sum)
    grad_qn, grad_kn, grad_v = lax.map(per_head, (query_b, key_b, value_b, grad_out))
    grad_qn = jnp.transpose(grad_qn, (1, 0, 2))
    grad_kn = jnp.transpose(grad_kn, (1, 0, 2))
    grad_v = jnp.transpose(grad_v, (1, 0, 2))
    grad_q = unnorm(grad_qn, query_raw, query_inv, gains[0])
    grad_k = unnorm(grad_kn, key_raw, key_inv, gains[1])
    grad_proj = jnp.concatenate([grad_q.reshape(TOKENS, HID), grad_k.reshape(TOKENS, HID), grad_v.reshape(TOKENS, HID)], 1).astype(jnp.bfloat16)

    def add_group(running, slices):
        rows_x, rows_d, rows_c = slices
        masked = jnp.concatenate([rows_d * (rows_c == clip_no).astype(jnp.bfloat16)[:, None] for clip_no in range(CLIPS)], 1)
        partial_sum = jnp.dot(rows_x.T, masked, preferred_element_type=jnp.float32)
        return (running + lax.optimization_barrier(partial_sum.astype(jnp.bfloat16)).astype(jnp.float32), None)
    start_sum = jnp.zeros((D, CLIPS * 3 * HID), jnp.float32)
    per_clip, unused = lax.scan(add_group, start_sum, (tokens.reshape(N_SEQ, TOK_DEV, D), grad_proj.reshape(N_SEQ, TOK_DEV, 3 * HID), token_clip.reshape(N_SEQ, TOK_DEV)))
    fisher = lax.optimization_barrier(jnp.sum(jnp.square(per_clip.reshape(D, CLIPS, 3, HID)), 1))
    fisher = jnp.transpose(fisher, (1, 0, 2))
    fisher_mean = jnp.sum(fisher) / (3 * D * HID)
    fisher_ratio = fisher / (fisher_mean + 1e-06)
    dampened = (w_qkv.astype(jnp.float32) / (1.0 + damp_mask.astype(jnp.float32)[None] * fisher_ratio)).astype(jnp.bfloat16)
    return (fisher_ratio, dampened)
```

```python
import functools
import math

import jax
import jax.numpy as jnp
from jax import lax
from jax.experimental import pallas as pl
from jax.experimental.pallas import tpu as pltpu
from jax.sharding import PartitionSpec as P

D = 3072
HD = 128
HEADS = 16
CLIPS = 3
EPS = 1e-6
AXES = ("seq", "head")


def normed(values, gain_row, head_count):
    shaped = values.reshape(values.shape[0], head_count, HD)
    inverse = lax.rsqrt(jnp.mean(shaped * shaped, -1, keepdims=True) + EPS)
    return (shaped * inverse * gain_row.reshape(head_count, HD), inverse, shaped)


def unnorm(upstream, shaped, inverse, gain_row, head_count):
    gain_grid = gain_row.reshape(head_count, HD)
    cubed = inverse * inverse * inverse
    return inverse * gain_grid * upstream - shaped * cubed * jnp.mean(
        shaped * gain_grid * upstream, -1, keepdims=True
    )


def by_clip(grad_rows, clip_ids):
    return jnp.concatenate(
        [
            grad_rows * (clip_ids == clip_no).astype(jnp.bfloat16)[..., None]
            for clip_no in range(CLIPS)
        ],
        -1,
    )


def row_sharded(tokens, w_qkv, gains, cotangent, token_clip, key_live, damp_mask):
    tok_rows = tokens.shape[0]
    width_dev = w_qkv.shape[2]
    rows_dev = w_qkv.shape[1]
    head_count = width_dev // HD
    all_tokens = token_clip.shape[0]
    seq_rank = lax.axis_index("seq")
    score_scale = 1.0 / math.sqrt(HD)
    projected = jnp.einsum(
        "tr,jrc->jtc",
        tokens,
        lax.all_gather(w_qkv, "seq", axis=1, tiled=True),
        preferred_element_type=jnp.float32,
    )
    query_n, query_inv, query_raw = normed(projected[0], gains[0], head_count)
    key_n, key_inv, key_raw = normed(projected[1], gains[1], head_count)
    query_b = query_n.astype(jnp.bfloat16)
    local_kv = jnp.concatenate(
        [
            key_n.astype(jnp.bfloat16).reshape(tok_rows, width_dev),
            projected[2].astype(jnp.bfloat16),
        ],
        1,
    )
    all_kv = lax.all_gather(local_kv, "seq", axis=0, tiled=True)
    keys_all = all_kv[:, :width_dev].reshape(all_tokens, head_count, HD)
    values_all = all_kv[:, width_dev:].reshape(all_tokens, head_count, HD)
    first_row = seq_rank * tok_rows
    clip_here = lax.dynamic_slice_in_dim(token_clip, first_row, tok_rows)
    positions = first_row + jnp.arange(tok_rows, dtype=jnp.int32)
    key_positions = jnp.arange(all_tokens, dtype=jnp.int32)
    allowed = (clip_here[:, None] == token_clip[None, :]) & (
        (key_live[None, :] == 1) | (positions[:, None] == key_positions[None, :])
    )
    scores = (
        jnp.einsum("thd,khd->htk", query_b, keys_all, preferred_element_type=jnp.float32)
        * score_scale
    )
    scores = jnp.where(allowed[None], scores, -1e30)
    peak = jnp.max(scores, -1, keepdims=True)
    expd = jnp.exp(scores - peak)
    probs = expd / jnp.sum(expd, -1, keepdims=True)
    grad_out = cotangent.reshape(tok_rows, head_count, HD)
    grad_p = jnp.einsum("thd,khd->htk", grad_out, values_all, preferred_element_type=jnp.float32)
    row_dot = jnp.sum(probs * grad_p, -1, keepdims=True)
    ds_half = (probs * (grad_p - row_dot)).astype(jnp.bfloat16)
    probs_half = probs.astype(jnp.bfloat16)
    grad_qn = (
        jnp.einsum("htk,khd->thd", ds_half, keys_all, preferred_element_type=jnp.float32)
        * score_scale
    )
    key_part = (
        jnp.einsum("htk,thd->khd", ds_half, query_b, preferred_element_type=jnp.float32)
        * score_scale
    )
    value_part = jnp.einsum(
        "htk,thd->khd", probs_half, grad_out, preferred_element_type=jnp.float32
    )
    key_terms = jnp.concatenate(
        [key_part.reshape(all_tokens, width_dev), value_part.reshape(all_tokens, width_dev)], 1
    )
    summed = lax.psum_scatter(
        key_terms.astype(jnp.bfloat16), "seq", scatter_dimension=0, tiled=True
    ).astype(jnp.float32)
    grad_q = unnorm(grad_qn, query_raw, query_inv, gains[0], head_count)
    grad_k = unnorm(
        summed[:, :width_dev].reshape(tok_rows, head_count, HD),
        key_raw,
        key_inv,
        gains[1],
        head_count,
    )
    grad_proj = jnp.concatenate(
        [
            grad_q.reshape(tok_rows, width_dev),
            grad_k.reshape(tok_rows, width_dev),
            summed[:, width_dev:],
        ],
        1,
    ).astype(jnp.bfloat16)
    masked = by_clip(grad_proj, clip_here)
    per_clip = lax.psum_scatter(
        lax.dot_general(
            tokens, masked, (((0,), (0,)), ((), ())), preferred_element_type=jnp.float32
        ).astype(jnp.bfloat16),
        "seq",
        scatter_dimension=0,
        tiled=True,
    ).astype(jnp.float32)
    fisher = jnp.sum(jnp.square(per_clip.reshape(rows_dev, CLIPS, 3, width_dev)), 1)
    fisher = jnp.transpose(fisher, (1, 0, 2))
    fisher_sum = lax.psum(jnp.sum(fisher), AXES)
    fisher_mean = fisher_sum / (3 * D * HEADS * HD)
    fisher_ratio = fisher / (fisher_mean + EPS)
    dampened = (
        w_qkv.astype(jnp.float32) / (1.0 + damp_mask.astype(jnp.float32)[None] * fisher_ratio)
    ).astype(jnp.bfloat16)
    return (fisher_ratio, dampened)


def project_kernel(nb, tb, rows, quarter, place, *refs):
    chunks = refs[:nb]
    pieces = refs[nb : nb + quarter]
    out32, out16 = refs[nb + quarter : nb + quarter + 2]
    xs, ws, xsem, wsem = refs[nb + quarter + 2 :]
    wcopies = []
    for k in range(quarter):
        start = pl.multiple_of(place[nb + k] * rows, rows)
        for j in range(3):
            wcopies.append(
                pltpu.make_async_copy(
                    pieces[k].at[pl.ds(j * rows, rows)],
                    ws.at[pl.ds(start, rows), pl.ds(j * HD, HD)],
                    wsem.at[k, j],
                )
            )
    xcopies = [
        pltpu.make_async_copy(chunks[b], xs.at[b], xsem.at[b]) for b in range(nb)
    ]
    for copy in wcopies:
        copy.start()
    for copy in xcopies:
        copy.start()
    for copy in wcopies:
        copy.wait()
    for b in range(nb):
        xcopies[b].wait()
        part = jnp.dot(xs[b], ws[...], preferred_element_type=jnp.float32)
        here = pl.ds(pl.multiple_of(place[b] * tb, tb), tb)
        out32[here, :] = part
        out16[here, :] = part.astype(jnp.bfloat16)


def head_kernel(nb, tb, rows, quarter, place, edges, *refs):
    chunks = refs[:nb]
    cots = refs[nb : nb + quarter]
    cot_other, mine, other, gain, clip_row, key_code = refs[nb + quarter : nb + quarter + 6]
    fisher_out, sum_out = refs[nb + quarter + 6 : nb + quarter + 8]
    (xs, do, proj, qn, kn, vb, qn_t, kn_t, do_t, es, dps, dk, dv, dproj, grads, xsem, csem) = refs[
        nb + quarter + 8 :
    ]
    scale = 1.0 / math.sqrt(HD)
    cot_copies = []
    for k in range(quarter):
        for side in range(2):
            src = (
                cots[k].at[pl.ds(3 * rows, tb)]
                if side == 0
                else cot_other.at[pl.ds(k * tb, tb)]
            )
            block = place[nb + quarter * (1 + side) + k]
            cot_copies.append(
                pltpu.make_async_copy(
                    src, do.at[pl.ds(pl.multiple_of(block * tb, tb), tb)], csem.at[side, k]
                )
            )
    xcopies = [
        pltpu.make_async_copy(
            chunks[b], xs.at[pl.ds(pl.multiple_of(place[b] * tb, tb), tb)], xsem.at[b]
        )
        for b in range(nb)
    ]
    for copy in cot_copies + xcopies:
        copy.start()

    def normalise(b, carry):
        here = pl.ds(pl.multiple_of(b * tb, tb), tb)
        total = mine[here, :] + other[here, :].astype(jnp.float32)
        proj[here, :] = total[:, : 2 * HD]
        for j, (flat, turned) in enumerate(((qn, qn_t), (kn, kn_t))):
            raw = total[:, j * HD : (j + 1) * HD]
            inv = lax.rsqrt(jnp.mean(raw * raw, -1, keepdims=True) + EPS)
            value = raw * inv * gain[j : j + 1, :]
            flat[here, :] = value.astype(jnp.bfloat16)
            turned[b] = value.T.astype(jnp.bfloat16)
        vb[here, :] = total[:, 2 * HD :].astype(jnp.bfloat16)
        return carry

    lax.fori_loop(0, nb, normalise, 0)
    for copy in cot_copies:
        copy.wait()

    def prepare(b, carry):
        here = pl.ds(pl.multiple_of(b * tb, tb), tb)
        do_t[b] = do[here, :].astype(jnp.float32).T.astype(jnp.bfloat16)
        dk[here, :] = jnp.zeros((tb, HD), jnp.float32)
        dv[here, :] = jnp.zeros((tb, HD), jnp.float32)
        return carry

    lax.fori_loop(0, nb, prepare, 0)

    def backward_norm(upstream, here, j):
        raw = proj[here, j * HD : (j + 1) * HD]
        inv = lax.rsqrt(jnp.mean(raw * raw, -1, keepdims=True) + EPS)
        weighted = gain[j : j + 1, :] * upstream
        cubed = inv * inv * inv
        return inv * weighted - raw * (cubed * jnp.mean(raw * weighted, -1, keepdims=True))

    offset = lax.broadcasted_iota(jnp.int32, (tb, tb), 0) - lax.broadcasted_iota(
        jnp.int32, (tb, tb), 1
    )

    def queries(i, carry):
        rows_q = pl.ds(pl.multiple_of(i * tb, tb), tb)
        q_t = qn_t[i]
        d_t = do_t[i]
        clip_q = clip_row[i]
        first, last = edges[i], edges[nb + i]

        def overlap(j):
            return (edges[j] <= last) & (edges[nb + j] >= first)

        def forward(j, sums):
            def tile():
                here = pl.ds(pl.multiple_of(j * tb, tb), tb)
                s = jnp.dot(kn[here, :], q_t, preferred_element_type=jnp.float32)
                allowed = (key_code[here, :] == clip_q) | (offset == (i - j) * tb)
                e = jnp.where(allowed, jnp.exp2(s * (scale * math.log2(math.e))), 0.0)
                dp = jnp.dot(vb[here, :], d_t, preferred_element_type=jnp.float32)
                es[here, :] = e
                dps[here, :] = dp
                return (
                    sums[0] + jnp.sum(e.reshape(tb // 8, 8, tb), 0),
                    sums[1] + jnp.sum((e * dp).reshape(tb // 8, 8, tb), 0),
                )

            return lax.cond(overlap(j), tile, lambda: sums)

        zero = jnp.zeros((8, tb), jnp.float32)
        sum_e, sum_edp = lax.fori_loop(0, nb, forward, (zero, zero))
        inv_l = 1.0 / jnp.sum(sum_e, 0, keepdims=True)
        row_dot = jnp.sum(sum_edp, 0, keepdims=True) * inv_l
        q_b = qn[rows_q, :]
        d_b = do[rows_q, :]

        def backward(j, dq_t):
            def tile():
                here = pl.ds(pl.multiple_of(j * tb, tb), tb)
                p = es[here, :] * inv_l
                ds = (p * (dps[here, :] - row_dot)).astype(jnp.bfloat16)
                dv[here, :] += jnp.dot(
                    p.astype(jnp.bfloat16), d_b, preferred_element_type=jnp.float32
                )
                dk[here, :] += jnp.dot(ds, q_b, preferred_element_type=jnp.float32)
                return dq_t + jnp.dot(kn_t[j], ds, preferred_element_type=jnp.float32)

            return lax.cond(overlap(j), tile, lambda: dq_t)

        dq_t = lax.fori_loop(0, nb, backward, jnp.zeros((HD, tb), jnp.float32))
        dproj[rows_q, :HD] = backward_norm(dq_t.T * scale, rows_q, 0).astype(jnp.bfloat16)
        return carry

    lax.fori_loop(0, nb, queries, 0)

    def keys(b, carry):
        here = pl.ds(pl.multiple_of(b * tb, tb), tb)
        dproj[here, HD : 2 * HD] = backward_norm(dk[here, :] * scale, here, 1).astype(jnp.bfloat16)
        dproj[here, 2 * HD :] = dv[here, :].astype(jnp.bfloat16)
        return carry

    lax.fori_loop(0, nb, keys, 0)
    grads[...] = jnp.zeros_like(grads)
    for copy in xcopies:
        copy.wait()

    def gradient(b, carry):
        here = pl.ds(pl.multiple_of(b * tb, tb), tb)
        turned = dproj[here, :].astype(jnp.float32).T

        def one_clip(clip, carry):
            part = jnp.where(clip_row[b] == clip, turned, 0.0).astype(jnp.bfloat16)
            grads[clip] += jnp.dot(part, xs[here, :], preferred_element_type=jnp.float32)
            return carry

        lax.fori_loop(edges[b], edges[nb + b] + 1, one_clip, 0)
        return carry

    lax.fori_loop(0, nb, gradient, 0)
    running = jnp.zeros((HD, rows), jnp.float32)
    for block in range(quarter):
        slot = place[nb + 3 * quarter + block]
        for j in range(3):
            span = (pl.ds(j * HD, HD), pl.ds(block * rows, rows))
            squares = jnp.zeros((HD, rows), jnp.float32)
            for clip in range(CLIPS):
                g = grads[clip, span[0], span[1]]
                squares += g * g
            running += squares
            fisher_out[slot, j * rows : (j + 1) * rows, :] = squares.T.astype(jnp.bfloat16)
    sum_out[...] = jnp.full((8, HD), jnp.sum(running), jnp.float32)


def finish_kernel(quarter, rows, shift, *refs):
    pieces = refs[:quarter]
    total, w, mask, ratio_out, damp_out = refs[quarter:]
    lane = pl.program_id(0)
    mean = total[0, 0] * (1.0 / (3 * D * HEADS * HD))
    factor = 1.0 / jnp.full((1, HD), mean + EPS, jnp.float32)
    damp = mask[...].astype(jnp.float32)
    for k in range(quarter):

        @pl.when(lax.rem(shift[0] + k, quarter) == lane)
        def _():
            for j in range(3):
                ratio = pieces[k][j * rows : (j + 1) * rows, :].astype(jnp.float32) * factor
                ratio_out[j] = ratio
                damp_out[j] = (w[j].astype(jnp.float32) / (1.0 + damp * ratio)).astype(
                    jnp.bfloat16
                )


def chip_per_head(tokens, w_qkv, gains, cotangent, token_clip, key_live, damp_mask, *, ns, nh):
    tb, width = tokens.shape
    rows, cols = w_qkv.shape[1:]
    quarter = cols // HD
    half = width // 2
    all_tokens = token_clip.shape[0]
    s = lax.axis_index("seq")
    h = lax.axis_index("head")
    core = h % 2
    vmem = pl.BlockSpec(memory_space=pltpu.VMEM)
    smem = pl.BlockSpec(memory_space=pltpu.SMEM)
    hbm = pl.BlockSpec(memory_space=pl.ANY)

    def index(si, hi):
        return si * nh + hi

    swap = [(index(a, b), index(a, b ^ 1)) for a in range(ns) for b in range(nh)]
    out_perms = []
    for k in range(quarter):
        out_perms.append(
            [
                (index(a, b), index((b % 2) * quarter + (k + a) % quarter, b - b % 2 + a // quarter))
                for a in range(ns)
                for b in range(nh)
            ]
        )
    back_perms = [[(b, a) for a, b in perm] for perm in out_perms]

    gains_other = lax.ppermute(gains, AXES, swap)
    pieces = []
    for k in range(quarter):
        col = ((k + s) % quarter) * HD
        piece = jnp.concatenate(
            [
                lax.dynamic_slice_in_dim(w_qkv, col, HD, 2).reshape(3 * rows, HD),
                lax.dynamic_slice_in_dim(cotangent, col, HD, 1),
            ],
            0,
        )
        pieces.append(lax.ppermute(piece, AXES, out_perms[k]))

    ring = list(range(0, ns, 2)) + list(range(1, ns, 2))[::-1]
    forth = [(ring[i], ring[(i + 1) % ns]) for i in range(ns)]
    back = [(b, a) for a, b in forth]
    position = [ring.index(i) for i in range(ns)]
    mine = lax.dynamic_slice_in_dim(tokens, core * half, half, 1)
    chunks, steps = [mine], [0]
    ahead = behind = mine
    for step in range(1, ns // 2):
        ahead = lax.ppermute(ahead, "seq", forth)
        behind = lax.ppermute(behind, "seq", back)
        chunks += [ahead, behind]
        steps += [-step, step]
    chunks.append(
        jnp.concatenate(
            [
                lax.ppermute(ahead[: tb // 2], "seq", forth),
                lax.ppermute(behind[tb // 2 :], "seq", back),
            ],
            0,
        )
    )
    steps.append(ns // 2)
    order = jnp.array([[ring[(position[i] + d) % ns] for d in steps] for i in range(ns)], jnp.int32)
    ks = jnp.arange(quarter, dtype=jnp.int32)
    row_block = (s - ks) % quarter
    place = jnp.concatenate(
        [
            lax.dynamic_index_in_dim(order, s, 0, False),
            row_block,
            row_block + core * quarter,
            row_block + (1 - core) * quarter,
            (s - ks) % quarter,
        ]
    ).astype(jnp.int32)

    cot_mine = jnp.concatenate([p[3 * rows :] for p in pieces], 0)
    cot_other = lax.ppermute(cot_mine, AXES, swap)

    params = pltpu.CompilerParams(vmem_limit_bytes=56 * 1024 * 1024)
    bf16, f32 = jnp.bfloat16, jnp.float32
    part32, part16 = pl.pallas_call(
        functools.partial(project_kernel, ns, tb, rows, quarter),
        out_shape=(
            jax.ShapeDtypeStruct((all_tokens, 3 * HD), f32),
            jax.ShapeDtypeStruct((all_tokens, 3 * HD), bf16),
        ),
        in_specs=[smem] + [hbm] * (ns + quarter),
        out_specs=(vmem, vmem),
        scratch_shapes=[
            pltpu.VMEM((ns, tb, half), bf16),
            pltpu.VMEM((half, 3 * HD), bf16),
            pltpu.SemaphoreType.DMA((ns,)),
            pltpu.SemaphoreType.DMA((quarter, 3)),
        ],
        compiler_params=params,
        name="project",
    )(place, *chunks, *pieces)
    other = lax.ppermute(part16, AXES, swap)

    own_gain = (s // quarter) == core
    gain = lax.dynamic_slice_in_dim(
        jnp.where(own_gain, gains, gains_other), (s % quarter) * HD, HD, 1
    )
    clip_row = token_clip.reshape(ns, 1, tb)
    key_code = jnp.where(key_live == 1, token_clip, -1)[:, None]
    blocks = token_clip.reshape(ns, tb)
    edges = jnp.concatenate([blocks[:, 0], blocks[:, -1]])
    fisher, part_sum = pl.pallas_call(
        functools.partial(head_kernel, ns, tb, rows, quarter),
        out_shape=(
            jax.ShapeDtypeStruct((quarter, 3 * rows, HD), bf16),
            jax.ShapeDtypeStruct((8, HD), f32),
        ),
        in_specs=[smem, smem] + [hbm] * (ns + quarter + 1) + [vmem] * 5,
        out_specs=(vmem, vmem),
        scratch_shapes=[
            pltpu.VMEM((all_tokens, half), bf16),
            pltpu.VMEM((all_tokens, HD), bf16),
            pltpu.VMEM((all_tokens, 2 * HD), f32),
            pltpu.VMEM((all_tokens, HD), bf16),
            pltpu.VMEM((all_tokens, HD), bf16),
            pltpu.VMEM((all_tokens, HD), bf16),
            pltpu.VMEM((ns, HD, tb), bf16),
            pltpu.VMEM((ns, HD, tb), bf16),
            pltpu.VMEM((ns, HD, tb), bf16),
            pltpu.VMEM((all_tokens, tb), f32),
            pltpu.VMEM((all_tokens, tb), f32),
            pltpu.VMEM((all_tokens, HD), f32),
            pltpu.VMEM((all_tokens, HD), f32),
            pltpu.VMEM((all_tokens, 3 * HD), bf16),
            pltpu.VMEM((CLIPS, 3 * HD, half), f32),
            pltpu.SemaphoreType.DMA((ns,)),
            pltpu.SemaphoreType.DMA((2, quarter)),
        ],
        compiler_params=params,
        name="head",
    )(place, edges, *chunks, *pieces, cot_other, part32, other, gain, clip_row, key_code)

    returned = [lax.ppermute(fisher[k], AXES, back_perms[k]) for k in range(quarter)]
    total = part_sum[:1]
    bit = 1
    while bit < nh:
        total = total + lax.ppermute(total, "head", [(i, i ^ bit) for i in range(nh)])
        bit *= 2
    bit = 1
    while bit < ns:
        total = total + lax.ppermute(total, "seq", [(i, i ^ bit) for i in range(ns)])
        bit *= 2
    shift = (s % quarter).astype(jnp.int32).reshape(1)
    full = lambda i, shift: (0, 0)
    lanes = lambda i, shift: (0, 0, i)
    return pl.pallas_call(
        functools.partial(finish_kernel, quarter, rows),
        out_shape=(
            jax.ShapeDtypeStruct((3, rows, cols), f32),
            jax.ShapeDtypeStruct((3, rows, cols), bf16),
        ),
        grid_spec=pltpu.PrefetchScalarGridSpec(
            num_scalar_prefetch=1,
            grid=(quarter,),
            in_specs=[pl.BlockSpec((3 * rows, HD), full)] * quarter
            + [
                pl.BlockSpec((1, HD), full, memory_space=pltpu.SMEM),
                pl.BlockSpec((3, rows, HD), lanes),
                pl.BlockSpec((rows, HD), lambda i, shift: (0, i)),
            ],
            out_specs=(
                pl.BlockSpec((3, rows, HD), lanes),
                pl.BlockSpec((3, rows, HD), lanes),
            ),
        ),
        compiler_params=params,
        name="finish",
    )(shift, *returned, total, w_qkv, damp_mask)


def solution(mesh):
    ns, nh = mesh.shape["seq"], mesh.shape["head"]

    def on_device(*args):
        if ns == 2 * (args[1].shape[2] // HD) and ns & (ns - 1) == 0 and nh % 2 == 0:
            return chip_per_head(*args, ns=ns, nh=nh)
        return row_sharded(*args)

    return jax.shard_map(
        on_device,
        mesh=mesh,
        in_specs=(
            P("seq", None),
            P(None, "seq", "head"),
            P(None, "head"),
            P("seq", "head"),
            P(),
            P(),
            P("seq", "head"),
        ),
        out_specs=(P(None, "seq", "head"), P(None, "seq", "head")),
        check_vma=False,
    )
```

```python
import functools
import math

import jax
import jax.numpy as jnp
from jax import lax
from jax.experimental import pallas as pl
from jax.experimental.pallas import tpu as pltpu
from jax.sharding import PartitionSpec as P

D = 3072
HD = 128
HEADS = 16
CLIPS = 3
EPS = 1e-6
VMEM_BYTES = 56 * 1024 * 1024
AXES = ("seq", "head")


def normed(values, gain_row, head_count):
    shaped = values.reshape(values.shape[0], head_count, HD)
    inverse = lax.rsqrt(jnp.mean(shaped * shaped, -1, keepdims=True) + EPS)
    return (shaped * inverse * gain_row.reshape(head_count, HD), inverse, shaped)


def unnorm(upstream, shaped, inverse, gain_row, head_count):
    gain_grid = gain_row.reshape(head_count, HD)
    cubed = inverse * inverse * inverse
    return inverse * gain_grid * upstream - shaped * cubed * jnp.mean(
        shaped * gain_grid * upstream, -1, keepdims=True
    )


def by_clip(grad_rows, clip_ids):
    return jnp.concatenate(
        [
            grad_rows * (clip_ids == clip_no).astype(jnp.bfloat16)[..., None]
            for clip_no in range(CLIPS)
        ],
        -1,
    )


def row_sharded(tokens, w_qkv, gains, cotangent, token_clip, key_live, damp_mask):
    tok_rows = tokens.shape[0]
    width_dev = w_qkv.shape[2]
    rows_dev = w_qkv.shape[1]
    head_count = width_dev // HD
    all_tokens = token_clip.shape[0]
    seq_rank = lax.axis_index("seq")
    score_scale = 1.0 / math.sqrt(HD)
    projected = jnp.einsum(
        "tr,jrc->jtc",
        tokens,
        lax.all_gather(w_qkv, "seq", axis=1, tiled=True),
        preferred_element_type=jnp.float32,
    )
    query_n, query_inv, query_raw = normed(projected[0], gains[0], head_count)
    key_n, key_inv, key_raw = normed(projected[1], gains[1], head_count)
    query_b = query_n.astype(jnp.bfloat16)
    local_kv = jnp.concatenate(
        [
            key_n.astype(jnp.bfloat16).reshape(tok_rows, width_dev),
            projected[2].astype(jnp.bfloat16),
        ],
        1,
    )
    all_kv = lax.all_gather(local_kv, "seq", axis=0, tiled=True)
    keys_all = all_kv[:, :width_dev].reshape(all_tokens, head_count, HD)
    values_all = all_kv[:, width_dev:].reshape(all_tokens, head_count, HD)
    first_row = seq_rank * tok_rows
    clip_here = lax.dynamic_slice_in_dim(token_clip, first_row, tok_rows)
    positions = first_row + jnp.arange(tok_rows, dtype=jnp.int32)
    key_positions = jnp.arange(all_tokens, dtype=jnp.int32)
    allowed = (clip_here[:, None] == token_clip[None, :]) & (
        (key_live[None, :] == 1) | (positions[:, None] == key_positions[None, :])
    )
    scores = (
        jnp.einsum("thd,khd->htk", query_b, keys_all, preferred_element_type=jnp.float32)
        * score_scale
    )
    scores = jnp.where(allowed[None], scores, -1e30)
    peak = jnp.max(scores, -1, keepdims=True)
    expd = jnp.exp(scores - peak)
    probs = expd / jnp.sum(expd, -1, keepdims=True)
    grad_out = cotangent.reshape(tok_rows, head_count, HD)
    grad_p = jnp.einsum("thd,khd->htk", grad_out, values_all, preferred_element_type=jnp.float32)
    row_dot = jnp.sum(probs * grad_p, -1, keepdims=True)
    ds_half = (probs * (grad_p - row_dot)).astype(jnp.bfloat16)
    probs_half = probs.astype(jnp.bfloat16)
    grad_qn = (
        jnp.einsum("htk,khd->thd", ds_half, keys_all, preferred_element_type=jnp.float32)
        * score_scale
    )
    key_part = (
        jnp.einsum("htk,thd->khd", ds_half, query_b, preferred_element_type=jnp.float32)
        * score_scale
    )
    value_part = jnp.einsum(
        "htk,thd->khd", probs_half, grad_out, preferred_element_type=jnp.float32
    )
    key_terms = jnp.concatenate(
        [key_part.reshape(all_tokens, width_dev), value_part.reshape(all_tokens, width_dev)], 1
    )
    summed = lax.psum_scatter(
        key_terms.astype(jnp.bfloat16), "seq", scatter_dimension=0, tiled=True
    ).astype(jnp.float32)
    grad_q = unnorm(grad_qn, query_raw, query_inv, gains[0], head_count)
    grad_k = unnorm(
        summed[:, :width_dev].reshape(tok_rows, head_count, HD),
        key_raw,
        key_inv,
        gains[1],
        head_count,
    )
    grad_proj = jnp.concatenate(
        [
            grad_q.reshape(tok_rows, width_dev),
            grad_k.reshape(tok_rows, width_dev),
            summed[:, width_dev:],
        ],
        1,
    ).astype(jnp.bfloat16)
    masked = by_clip(grad_proj, clip_here)
    per_clip = lax.psum_scatter(
        lax.dot_general(
            tokens, masked, (((0,), (0,)), ((), ())), preferred_element_type=jnp.float32
        ).astype(jnp.bfloat16),
        "seq",
        scatter_dimension=0,
        tiled=True,
    ).astype(jnp.float32)
    fisher = jnp.sum(jnp.square(per_clip.reshape(rows_dev, CLIPS, 3, width_dev)), 1)
    fisher = jnp.transpose(fisher, (1, 0, 2))
    fisher_sum = lax.psum(jnp.sum(fisher), AXES)
    fisher_mean = fisher_sum / (3 * D * HEADS * HD)
    fisher_ratio = fisher / (fisher_mean + EPS)
    dampened = (
        w_qkv.astype(jnp.float32) / (1.0 + damp_mask.astype(jnp.float32)[None] * fisher_ratio)
    ).astype(jnp.bfloat16)
    return (fisher_ratio, dampened)


def project_kernel(nb, tb, rows, quarter, with_cot, place, *refs):
    chunks = refs[:nb]
    pieces = refs[nb : nb + quarter]
    outs = refs[nb + quarter : -6]
    xs, ws, cs, xsem, wsem, csem = refs[-6:]
    copies = []
    for k in range(quarter):
        start = pl.multiple_of(place[k] * rows, rows)
        for j in range(3):
            copies.append(
                pltpu.make_async_copy(
                    pieces[k].at[pl.ds(j * rows, rows)],
                    ws.at[pl.ds(start, rows), pl.ds(j * HD, HD)],
                    wsem.at[k, j],
                )
            )
        if with_cot:
            copies.append(
                pltpu.make_async_copy(
                    pieces[k].at[pl.ds(3 * rows, tb)], cs.at[pl.ds(k * tb, tb)], csem.at[k]
                )
            )
    xcopies = []
    at = 0
    for b, chunk in enumerate(chunks):
        height = chunk.shape[0]
        xcopies.append(pltpu.make_async_copy(chunk, xs.at[pl.ds(at, height)], xsem.at[b]))
        at += height
    for copy in copies + xcopies:
        copy.start()
    for copy in copies:
        copy.wait()
    if with_cot:
        outs[2][...] = cs[...]
    for copy in xcopies:
        copy.wait()
    part = jnp.dot(xs[...], ws[...], preferred_element_type=jnp.float32)
    outs[0][...] = part
    outs[1][...] = part.astype(jnp.bfloat16)


def project(chunks, pieces, row_block, tb, with_cot):
    nb, quarter = len(chunks), len(pieces)
    half = chunks[0].shape[1]
    total = sum(chunk.shape[0] for chunk in chunks)
    rows = (pieces[0].shape[0] - tb) // 3
    vmem = pl.BlockSpec(memory_space=pltpu.VMEM)
    shapes = [
        jax.ShapeDtypeStruct((total, 3 * HD), jnp.float32),
        jax.ShapeDtypeStruct((total, 3 * HD), jnp.bfloat16),
    ]
    if with_cot:
        shapes.append(jax.ShapeDtypeStruct((quarter * tb, HD), jnp.bfloat16))
    return pl.pallas_call(
        functools.partial(project_kernel, nb, tb, rows, quarter, with_cot),
        out_shape=shapes,
        in_specs=[pl.BlockSpec(memory_space=pltpu.SMEM)]
        + [pl.BlockSpec(memory_space=pl.ANY)] * (nb + quarter),
        out_specs=[vmem] * len(shapes),
        scratch_shapes=[
            pltpu.VMEM((total, half), jnp.bfloat16),
            pltpu.VMEM((half, 3 * HD), jnp.bfloat16),
            pltpu.VMEM((quarter * tb, HD), jnp.bfloat16),
            pltpu.SemaphoreType.DMA((nb,)),
            pltpu.SemaphoreType.DMA((quarter, 3)),
            pltpu.SemaphoreType.DMA((quarter,)),
        ],
        compiler_params=pltpu.CompilerParams(vmem_limit_bytes=VMEM_BYTES),
        name="project",
    )(row_block, *chunks, *pieces)


def head_kernel(nb, tb, rows, quarter, parts, place, edges, *refs):
    chunks = refs[: 2 * nb]
    cots = refs[2 * nb : 2 * nb + 2]
    ends = 2 * nb + 2 + 2 * len(parts)
    projections = refs[2 * nb + 2 : ends]
    gain, clip_row, key_row = refs[ends : ends + 3]
    fisher_out = refs[ends + 3 : ends + 3 + quarter]
    sum_out = refs[ends + 3 + quarter]
    (xs, do, proj, qn, kn, vb, qn_t, kn_t, do_t, key_code, es, dps, dk, dv, dproj, grads) = refs[
        ends + 4 + quarter : -2
    ]
    xsem, csem = refs[-2:]
    scale = 1.0 / math.sqrt(HD)
    cot_copies = []
    for k in range(quarter):
        for side in range(2):
            src = cots[side].at[pl.ds(k * tb, tb)]
            block = place[nb + quarter * (1 + side) + k]
            cot_copies.append(
                pltpu.make_async_copy(
                    src, do.at[pl.ds(pl.multiple_of(block * tb, tb), tb)], csem.at[side, k]
                )
            )
    xcopies = [
        pltpu.make_async_copy(
            chunks[b],
            xs.at[pl.ds(pl.multiple_of(place[b // 2] * tb + b % 2 * (tb // 2), tb // 2), tb // 2)],
            xsem.at[b],
        )
        for b in range(2 * nb)
    ]
    for copy in cot_copies + xcopies:
        copy.start()

    first_block = 0
    for part, count in enumerate(parts):

        def normalise(b, carry, first_block=first_block, part=part):
            source = pl.ds(pl.multiple_of(b * tb, tb), tb)
            block = place[first_block + b]
            here = pl.ds(pl.multiple_of(block * tb, tb), tb)
            mine, other = projections[2 * part : 2 * part + 2]
            total = mine[source, :] + other[source, :].astype(jnp.float32)
            proj[here, :] = total[:, : 2 * HD]
            for j, (flat, turned) in enumerate(((qn, qn_t), (kn, kn_t))):
                raw = total[:, j * HD : (j + 1) * HD]
                inv = lax.rsqrt(jnp.mean(raw * raw, -1, keepdims=True) + EPS)
                value = raw * inv * gain[j : j + 1, :]
                flat[here, :] = value.astype(jnp.bfloat16)
                turned[block] = value.T.astype(jnp.bfloat16)
            vb[here, :] = total[:, 2 * HD :].astype(jnp.bfloat16)
            key_code[here, :] = jnp.broadcast_to(key_row[block], (HD, tb)).T
            return carry

        lax.fori_loop(0, count, normalise, 0)
        first_block += count
    for copy in cot_copies:
        copy.wait()

    def prepare(b, carry):
        here = pl.ds(pl.multiple_of(b * tb, tb), tb)
        do_t[b] = do[here, :].astype(jnp.float32).T.astype(jnp.bfloat16)
        dk[here, :] = jnp.zeros((tb, HD), jnp.float32)
        dv[here, :] = jnp.zeros((tb, HD), jnp.float32)
        return carry

    lax.fori_loop(0, nb, prepare, 0)

    def backward_norm(upstream, here, j):
        raw = proj[here, j * HD : (j + 1) * HD]
        inv = lax.rsqrt(jnp.mean(raw * raw, -1, keepdims=True) + EPS)
        weighted = gain[j : j + 1, :] * upstream
        cubed = inv * inv * inv
        return inv * weighted - raw * (cubed * jnp.mean(raw * weighted, -1, keepdims=True))

    wide = 2 * tb
    units = nb // 2
    offset = lax.broadcasted_iota(jnp.int32, (wide, tb), 0) - lax.broadcasted_iota(
        jnp.int32, (wide, tb), 1
    )

    def forward(i, unit, sums):
        here = pl.ds(unit * wide, wide)
        s = jnp.dot(kn[here, :], qn_t[i], preferred_element_type=jnp.float32)
        codes = jnp.concatenate([key_code[here, :]] * (tb // HD), 1)
        allowed = (codes == clip_row[i]) | (offset == i * tb - unit * wide)
        e = jnp.where(allowed, jnp.exp2(s * (scale * math.log2(math.e))), 0.0)
        dp = jnp.dot(vb[here, :], do_t[i], preferred_element_type=jnp.float32)
        es[here, :] = e
        dps[here, :] = dp
        return (
            sums[0] + jnp.sum(e.reshape(wide // 8, 8, tb), 0),
            sums[1] + jnp.sum((e * dp).reshape(wide // 8, 8, tb), 0),
        )

    def finish_sums(sums):
        inv_l = 1.0 / jnp.sum(sums[0], 0, keepdims=True)
        return inv_l, jnp.sum(sums[1], 0, keepdims=True) * inv_l

    def backward(i, unit, inv_l, row_dot, dq_t):
        here = pl.ds(unit * wide, wide)
        rows_q = pl.ds(pl.multiple_of(i * tb, tb), tb)
        p = es[here, :] * inv_l
        ds = (p * (dps[here, :] - row_dot)).astype(jnp.bfloat16)
        dv[here, :] += jnp.dot(
            p.astype(jnp.bfloat16), do[rows_q, :], preferred_element_type=jnp.float32
        )
        dk[here, :] += jnp.dot(ds, qn[rows_q, :], preferred_element_type=jnp.float32)
        return (
            dq_t
            + jnp.dot(kn_t[2 * unit], ds[:tb], preferred_element_type=jnp.float32)
            + jnp.dot(kn_t[2 * unit + 1], ds[tb:], preferred_element_type=jnp.float32)
        )

    def store_dq(i, dq_t):
        rows_q = pl.ds(pl.multiple_of(i * tb, tb), tb)
        dproj[rows_q, :HD] = backward_norm(dq_t.T * scale, rows_q, 0).astype(jnp.bfloat16)

    zero = jnp.zeros((8, tb), jnp.float32)

    def queries(i, carry):
        sums = (zero, zero)
        for unit in range(units):
            sums = forward(i, unit, sums)
        inv_l, row_dot = finish_sums(sums)
        dq_t = jnp.zeros((HD, tb), jnp.float32)
        for unit in range(units):
            dq_t = backward(i, unit, inv_l, row_dot, dq_t)
        store_dq(i, dq_t)
        return carry

    lax.fori_loop(0, nb, queries, 0)

    def keys(b, carry):
        here = pl.ds(pl.multiple_of(b * tb, tb), tb)
        dproj[here, HD : 2 * HD] = backward_norm(dk[here, :] * scale, here, 1).astype(jnp.bfloat16)
        dproj[here, 2 * HD :] = dv[here, :].astype(jnp.bfloat16)
        return carry

    lax.fori_loop(0, nb, keys, 0)
    grads[...] = jnp.zeros_like(grads)
    for copy in xcopies:
        copy.wait()

    def gradient(b, carry):
        here = pl.ds(pl.multiple_of(b * wide, wide), wide)
        turned = dproj[here, :].astype(jnp.float32).T
        clips = jnp.concatenate([clip_row[2 * b], clip_row[2 * b + 1]], 1)

        def one_clip(clip, carry):
            part = jnp.where(clips == clip, turned, 0.0).astype(jnp.bfloat16)
            grads[clip] += jnp.dot(part, xs[here, :], preferred_element_type=jnp.float32)
            return carry

        lax.fori_loop(edges[2 * b], edges[nb + 2 * b + 1] + 1, one_clip, 0)
        return carry

    lax.fori_loop(0, units, gradient, 0)
    running = jnp.zeros((HD, rows), jnp.float32)
    for k in range(quarter):
        block = place[nb + k]
        columns = pl.ds(pl.multiple_of(block * rows, rows), rows)
        for j in range(3):
            squares = jnp.zeros((HD, rows), jnp.float32)
            for clip in range(CLIPS):
                g = grads[clip, j * HD : (j + 1) * HD, columns]
                squares += g * g
            running += squares
            fisher_out[k][j * rows : (j + 1) * rows, :] = squares.T.astype(jnp.bfloat16)
    sum_out[...] = jnp.full((8, HD), jnp.sum(running), jnp.float32)


def finish_kernel(quarter, rows, shift, *refs):
    pieces = refs[:quarter]
    total, w, mask, ratio_out, damp_out = refs[quarter:]
    lane = pl.program_id(0)
    mean = total[0, 0] * (1.0 / (3 * D * HEADS * HD))
    factor = 1.0 / jnp.full((1, HD), mean + EPS, jnp.float32)
    damp = mask[...].astype(jnp.float32)
    for k in range(quarter):

        @pl.when(lax.rem(shift[0] + k, quarter) == lane)
        def _():
            for j in range(3):
                ratio = pieces[k][j * rows : (j + 1) * rows, :].astype(jnp.float32) * factor
                ratio_out[j] = ratio
                damp_out[j] = (w[j].astype(jnp.float32) / (1.0 + damp * ratio)).astype(
                    jnp.bfloat16
                )


def chip_per_head(tokens, w_qkv, gains, cotangent, token_clip, key_live, damp_mask, *, ns, nh):
    tb, width = tokens.shape
    rows, cols = w_qkv.shape[1:]
    quarter = cols // HD
    half = width // 2
    all_tokens = token_clip.shape[0]
    s = lax.axis_index("seq")
    h = lax.axis_index("head")
    core = h % 2
    vmem = pl.BlockSpec(memory_space=pltpu.VMEM)
    smem = pl.BlockSpec(memory_space=pltpu.SMEM)
    hbm = pl.BlockSpec(memory_space=pl.ANY)

    def index(si, hi):
        return si * nh + hi

    swap = [(index(a, b), index(a, b ^ 1)) for a in range(ns) for b in range(nh)]
    out_perms = []
    for k in range(quarter):
        out_perms.append(
            [
                (index(a, b), index((b % 2) * quarter + (k + a) % quarter, b - b % 2 + a // quarter))
                for a in range(ns)
                for b in range(nh)
            ]
        )
    back_perms = [[(b, a) for a, b in perm] for perm in out_perms]

    gains_other = lax.ppermute(gains, AXES, swap)
    outgoing = []
    for k in range(quarter):
        col = ((k + s) % quarter) * HD
        outgoing.append(
            jnp.concatenate(
                [
                    lax.dynamic_slice_in_dim(w_qkv, col, HD, 2).reshape(3 * rows, HD),
                    lax.dynamic_slice_in_dim(cotangent, col, HD, 1),
                ],
                0,
            )
        )
    pieces = []
    for k in range(0, quarter, 2):
        pair = outgoing[k : k + 2]
        if k:
            barred = lax.optimization_barrier((*pair, *pieces))
            pair, pieces = list(barred[: len(pair)]), list(barred[len(pair) :])
        pieces += [lax.ppermute(piece, AXES, out_perms[k + i]) for i, piece in enumerate(pair)]

    ring = list(range(0, ns, 2)) + list(range(1, ns, 2))[::-1]
    forth = [(ring[i], ring[(i + 1) % ns]) for i in range(ns)]
    back = [(b, a) for a, b in forth]
    position = [ring.index(i) for i in range(ns)]
    mine = lax.dynamic_slice_in_dim(tokens, core * half, half, 1)
    halves = [mine[: tb // 2], mine[tb // 2 :]]
    chunks, steps = list(halves), [0]
    ahead, behind = list(halves), list(halves)
    for step in range(1, ns // 2):
        ahead = [lax.ppermute(part, "seq", forth) for part in ahead]
        behind = [lax.ppermute(part, "seq", back) for part in behind]
        chunks += ahead + behind
        steps += [-step, step]
    chunks += [lax.ppermute(ahead[0], "seq", forth), lax.ppermute(behind[1], "seq", back)]
    steps.append(ns // 2)
    order = jnp.array([[ring[(position[i] + d) % ns] for d in steps] for i in range(ns)], jnp.int32)
    ks = jnp.arange(quarter, dtype=jnp.int32)
    row_block = ((s - ks) % quarter).astype(jnp.int32)
    place = jnp.concatenate(
        [
            lax.dynamic_index_in_dim(order, s, 0, False),
            row_block,
            row_block + core * quarter,
            row_block + (1 - core) * quarter,
        ]
    ).astype(jnp.int32)

    params = pltpu.CompilerParams(vmem_limit_bytes=VMEM_BYTES)
    bf16, f32 = jnp.bfloat16, jnp.float32
    own_gain = (s // quarter) == core
    gain = lax.dynamic_slice_in_dim(
        jnp.where(own_gain, gains, gains_other), (s % quarter) * HD, HD, 1
    )
    clip_row = token_clip.reshape(ns, 1, tb)
    key_row = jnp.where(key_live == 1, token_clip, -1).reshape(ns, 1, tb)
    blocks = token_clip.reshape(ns, tb)
    edges = jnp.concatenate([blocks[:, 0], blocks[:, -1]])
    place, row_block, edges, gain, clip_row, key_row, *pieces = lax.optimization_barrier(
        (place, row_block, edges, gain, clip_row, key_row, *pieces)
    )
    early = ns - 3
    first32, first16, cot_mine = project(chunks[: 2 * early], pieces, row_block, tb, True)
    first_other = lax.ppermute(first16, AXES, swap)
    cot_other = lax.ppermute(cot_mine, AXES, swap)
    last32, last16 = project(chunks[2 * early :], pieces, row_block, tb, False)
    last_other = lax.ppermute(last16, AXES, swap)

    *fisher, part_sum = pl.pallas_call(
        functools.partial(head_kernel, ns, tb, rows, quarter, (early, ns - early)),
        out_shape=(
            *[jax.ShapeDtypeStruct((3 * rows, HD), bf16)] * quarter,
            jax.ShapeDtypeStruct((8, HD), f32),
        ),
        in_specs=[smem, smem] + [hbm] * (2 * ns + 2) + [vmem] * 7,
        out_specs=[vmem] * (quarter + 1),
        scratch_shapes=[
            pltpu.VMEM((all_tokens, half), bf16),
            pltpu.VMEM((all_tokens, HD), bf16),
            pltpu.VMEM((all_tokens, 2 * HD), f32),
            pltpu.VMEM((all_tokens, HD), bf16),
            pltpu.VMEM((all_tokens, HD), bf16),
            pltpu.VMEM((all_tokens, HD), bf16),
            pltpu.VMEM((ns, HD, tb), bf16),
            pltpu.VMEM((ns, HD, tb), bf16),
            pltpu.VMEM((ns, HD, tb), bf16),
            pltpu.VMEM((all_tokens, HD), jnp.int32),
            pltpu.VMEM((all_tokens, tb), f32),
            pltpu.VMEM((all_tokens, tb), f32),
            pltpu.VMEM((all_tokens, HD), f32),
            pltpu.VMEM((all_tokens, HD), f32),
            pltpu.VMEM((all_tokens, 3 * HD), bf16),
            pltpu.VMEM((CLIPS, 3 * HD, half), f32),
            pltpu.SemaphoreType.DMA((2 * ns,)),
            pltpu.SemaphoreType.DMA((2, quarter)),
        ],
        compiler_params=params,
        name="head",
    )(
        place,
        edges,
        *chunks,
        cot_mine,
        cot_other,
        first32,
        first_other,
        last32,
        last_other,
        gain,
        clip_row,
        key_row,
    )

    returned = [lax.ppermute(fisher[k], AXES, back_perms[k]) for k in range(quarter)]
    total = part_sum[:1]
    bit = 1
    while bit < nh:
        total = total + lax.ppermute(total, "head", [(i, i ^ bit) for i in range(nh)])
        bit *= 2
    bit = 1
    while bit < ns:
        total = total + lax.ppermute(total, "seq", [(i, i ^ bit) for i in range(ns)])
        bit *= 2
    shift = (s % quarter).astype(jnp.int32).reshape(1)
    full = lambda i, shift: (0, 0)
    lanes = lambda i, shift: (0, 0, i)
    return pl.pallas_call(
        functools.partial(finish_kernel, quarter, rows),
        out_shape=(
            jax.ShapeDtypeStruct((3, rows, cols), f32),
            jax.ShapeDtypeStruct((3, rows, cols), bf16),
        ),
        grid_spec=pltpu.PrefetchScalarGridSpec(
            num_scalar_prefetch=1,
            grid=(quarter,),
            in_specs=[pl.BlockSpec((3 * rows, HD), full)] * quarter
            + [
                pl.BlockSpec((1, HD), full, memory_space=pltpu.SMEM),
                pl.BlockSpec((3, rows, HD), lanes),
                pl.BlockSpec((rows, HD), lambda i, shift: (0, i)),
            ],
            out_specs=(
                pl.BlockSpec((3, rows, HD), lanes),
                pl.BlockSpec((3, rows, HD), lanes),
            ),
        ),
        compiler_params=params,
        name="finish",
    )(shift, *returned, total, w_qkv, damp_mask)


def solution(mesh):
    ns, nh = mesh.shape["seq"], mesh.shape["head"]

    def on_device(*args):
        if ns == 2 * (args[1].shape[2] // HD) and ns & (ns - 1) == 0 and nh % 2 == 0:
            return chip_per_head(*args, ns=ns, nh=nh)
        return row_sharded(*args)

    return jax.shard_map(
        on_device,
        mesh=mesh,
        in_specs=(
            P("seq", None),
            P(None, "seq", "head"),
            P(None, "head"),
            P("seq", "head"),
            P(),
            P(),
            P("seq", "head"),
        ),
        out_specs=(P(None, "seq", "head"), P(None, "seq", "head")),
        check_vma=False,
    )
```

```python
import functools
import math

import jax
import jax.numpy as jnp
from jax import lax
from jax.experimental import pallas as pl
from jax.experimental.pallas import tpu as pltpu
from jax.sharding import PartitionSpec as P

D = 3072
HD = 128
HEADS = 16
CLIPS = 3
EPS = 1e-6
VMEM_BYTES = 56 * 1024 * 1024
AXES = ("seq", "head")


def normed(values, gain_row, head_count):
    shaped = values.reshape(values.shape[0], head_count, HD)
    inverse = lax.rsqrt(jnp.mean(shaped * shaped, -1, keepdims=True) + EPS)
    return (shaped * inverse * gain_row.reshape(head_count, HD), inverse, shaped)


def unnorm(upstream, shaped, inverse, gain_row, head_count):
    gain_grid = gain_row.reshape(head_count, HD)
    cubed = inverse * inverse * inverse
    return inverse * gain_grid * upstream - shaped * cubed * jnp.mean(
        shaped * gain_grid * upstream, -1, keepdims=True
    )


def by_clip(grad_rows, clip_ids):
    return jnp.concatenate(
        [
            grad_rows * (clip_ids == clip_no).astype(jnp.bfloat16)[..., None]
            for clip_no in range(CLIPS)
        ],
        -1,
    )


def row_sharded(tokens, w_qkv, gains, cotangent, token_clip, key_live, damp_mask):
    tok_rows = tokens.shape[0]
    width_dev = w_qkv.shape[2]
    rows_dev = w_qkv.shape[1]
    head_count = width_dev // HD
    all_tokens = token_clip.shape[0]
    seq_rank = lax.axis_index("seq")
    score_scale = 1.0 / math.sqrt(HD)
    projected = jnp.einsum(
        "tr,jrc->jtc",
        tokens,
        lax.all_gather(w_qkv, "seq", axis=1, tiled=True),
        preferred_element_type=jnp.float32,
    )
    query_n, query_inv, query_raw = normed(projected[0], gains[0], head_count)
    key_n, key_inv, key_raw = normed(projected[1], gains[1], head_count)
    query_b = query_n.astype(jnp.bfloat16)
    local_kv = jnp.concatenate(
        [
            key_n.astype(jnp.bfloat16).reshape(tok_rows, width_dev),
            projected[2].astype(jnp.bfloat16),
        ],
        1,
    )
    all_kv = lax.all_gather(local_kv, "seq", axis=0, tiled=True)
    keys_all = all_kv[:, :width_dev].reshape(all_tokens, head_count, HD)
    values_all = all_kv[:, width_dev:].reshape(all_tokens, head_count, HD)
    first_row = seq_rank * tok_rows
    clip_here = lax.dynamic_slice_in_dim(token_clip, first_row, tok_rows)
    positions = first_row + jnp.arange(tok_rows, dtype=jnp.int32)
    key_positions = jnp.arange(all_tokens, dtype=jnp.int32)
    allowed = (clip_here[:, None] == token_clip[None, :]) & (
        (key_live[None, :] == 1) | (positions[:, None] == key_positions[None, :])
    )
    scores = (
        jnp.einsum("thd,khd->htk", query_b, keys_all, preferred_element_type=jnp.float32)
        * score_scale
    )
    scores = jnp.where(allowed[None], scores, -1e30)
    peak = jnp.max(scores, -1, keepdims=True)
    expd = jnp.exp(scores - peak)
    probs = expd / jnp.sum(expd, -1, keepdims=True)
    grad_out = cotangent.reshape(tok_rows, head_count, HD)
    grad_p = jnp.einsum("thd,khd->htk", grad_out, values_all, preferred_element_type=jnp.float32)
    row_dot = jnp.sum(probs * grad_p, -1, keepdims=True)
    ds_half = (probs * (grad_p - row_dot)).astype(jnp.bfloat16)
    probs_half = probs.astype(jnp.bfloat16)
    grad_qn = (
        jnp.einsum("htk,khd->thd", ds_half, keys_all, preferred_element_type=jnp.float32)
        * score_scale
    )
    key_part = (
        jnp.einsum("htk,thd->khd", ds_half, query_b, preferred_element_type=jnp.float32)
        * score_scale
    )
    value_part = jnp.einsum(
        "htk,thd->khd", probs_half, grad_out, preferred_element_type=jnp.float32
    )
    key_terms = jnp.concatenate(
        [key_part.reshape(all_tokens, width_dev), value_part.reshape(all_tokens, width_dev)], 1
    )
    summed = lax.psum_scatter(
        key_terms.astype(jnp.bfloat16), "seq", scatter_dimension=0, tiled=True
    ).astype(jnp.float32)
    grad_q = unnorm(grad_qn, query_raw, query_inv, gains[0], head_count)
    grad_k = unnorm(
        summed[:, :width_dev].reshape(tok_rows, head_count, HD),
        key_raw,
        key_inv,
        gains[1],
        head_count,
    )
    grad_proj = jnp.concatenate(
        [
            grad_q.reshape(tok_rows, width_dev),
            grad_k.reshape(tok_rows, width_dev),
            summed[:, width_dev:],
        ],
        1,
    ).astype(jnp.bfloat16)
    masked = by_clip(grad_proj, clip_here)
    per_clip = lax.psum_scatter(
        lax.dot_general(
            tokens, masked, (((0,), (0,)), ((), ())), preferred_element_type=jnp.float32
        ).astype(jnp.bfloat16),
        "seq",
        scatter_dimension=0,
        tiled=True,
    ).astype(jnp.float32)
    fisher = jnp.sum(jnp.square(per_clip.reshape(rows_dev, CLIPS, 3, width_dev)), 1)
    fisher = jnp.transpose(fisher, (1, 0, 2))
    fisher_sum = lax.psum(jnp.sum(fisher), AXES)
    fisher_mean = fisher_sum / (3 * D * HEADS * HD)
    fisher_ratio = fisher / (fisher_mean + EPS)
    dampened = (
        w_qkv.astype(jnp.float32) / (1.0 + damp_mask.astype(jnp.float32)[None] * fisher_ratio)
    ).astype(jnp.bfloat16)
    return (fisher_ratio, dampened)


def project_kernel(nb, tb, rows, quarter, with_cot, place, *refs):
    chunks = refs[:nb]
    pieces = refs[nb : nb + quarter]
    outs = refs[nb + quarter : -6]
    xs, ws, cs, xsem, wsem, csem = refs[-6:]
    copies = []
    for k in range(quarter):
        start = pl.multiple_of(place[k] * rows, rows)
        for j in range(3):
            copies.append(
                pltpu.make_async_copy(
                    pieces[k].at[pl.ds(j * rows, rows)],
                    ws.at[pl.ds(start, rows), pl.ds(j * HD, HD)],
                    wsem.at[k, j],
                )
            )
        if with_cot:
            copies.append(
                pltpu.make_async_copy(
                    pieces[k].at[pl.ds(3 * rows, tb)], cs.at[pl.ds(k * tb, tb)], csem.at[k]
                )
            )
    xcopies = []
    at = 0
    for b, chunk in enumerate(chunks):
        height = chunk.shape[0]
        xcopies.append(pltpu.make_async_copy(chunk, xs.at[pl.ds(at, height)], xsem.at[b]))
        at += height
    for copy in copies + xcopies:
        copy.start()
    for copy in copies:
        copy.wait()
    if with_cot:
        outs[1][...] = cs[...]
    for copy in xcopies:
        copy.wait()
    part = jnp.dot(xs[...], ws[...], preferred_element_type=jnp.float32)
    outs[0][...] = part.astype(jnp.bfloat16)


def project(chunks, pieces, row_block, tb, with_cot):
    nb, quarter = len(chunks), len(pieces)
    half = chunks[0].shape[1]
    total = sum(chunk.shape[0] for chunk in chunks)
    rows = (pieces[0].shape[0] - tb) // 3
    vmem = pl.BlockSpec(memory_space=pltpu.VMEM)
    shapes = [
        jax.ShapeDtypeStruct((total, 3 * HD), jnp.bfloat16),
    ]
    if with_cot:
        shapes.append(jax.ShapeDtypeStruct((quarter * tb, HD), jnp.bfloat16))
    return pl.pallas_call(
        functools.partial(project_kernel, nb, tb, rows, quarter, with_cot),
        out_shape=shapes,
        in_specs=[pl.BlockSpec(memory_space=pltpu.SMEM)]
        + [pl.BlockSpec(memory_space=pl.ANY)] * (nb + quarter),
        out_specs=[vmem] * len(shapes),
        scratch_shapes=[
            pltpu.VMEM((total, half), jnp.bfloat16),
            pltpu.VMEM((half, 3 * HD), jnp.bfloat16),
            pltpu.VMEM((quarter * tb, HD), jnp.bfloat16),
            pltpu.SemaphoreType.DMA((nb,)),
            pltpu.SemaphoreType.DMA((quarter, 3)),
            pltpu.SemaphoreType.DMA((quarter,)),
        ],
        compiler_params=pltpu.CompilerParams(vmem_limit_bytes=VMEM_BYTES),
        cost_estimate=pl.CostEstimate(flops=8800000000, bytes_accessed=28800000, transcendentals=0),
        name="project",
    )(row_block, *chunks, *pieces)


def cover(total, unit):
    count = max(1, total // unit)
    return (unit,) * (count - 1) + (total - unit * (count - 1),)


def head_kernel(nb, tb, rows, quarter, parts, layout, spans, place, windows, *refs):
    nc = len(layout)
    chunks = refs[:nc]
    cots = refs[nc : nc + 2]
    ends = nc + 2 + 2 * len(parts)
    projections = refs[nc + 2 : ends]
    gain, clip_row, key_row, clips = refs[ends : ends + 4]
    fisher_out = refs[ends + 4 : ends + 4 + quarter]
    sum_out = refs[ends + 4 + quarter]
    (do, q_raw_t, k_raw, qn, kn, vb, qn_t, kn_t, do_t, key_code, es, dps, dk, dv) = refs[
        ends + 5 + quarter : -5
    ]
    dproj_t, xs, squares, xsem, csem = refs[-5:]
    scale = 1.0 / math.sqrt(HD)
    cot_copies = []
    for k in range(quarter):
        for side in range(2):
            src = cots[side].at[pl.ds(k * tb, tb)]
            block = place[nb + quarter * (1 + side) + k]
            cot_copies.append(
                pltpu.make_async_copy(
                    src, do.at[pl.ds(pl.multiple_of(block * tb, tb), tb)], csem.at[side, k]
                )
            )
    xcopies = []
    for b, (block, offset, count) in enumerate(layout):
        start = pl.multiple_of(place[block] * tb + offset, count)
        xcopies.append(pltpu.make_async_copy(chunks[b], xs.at[pl.ds(start, count)], xsem.at[b]))
    for copy in cot_copies + xcopies:
        copy.start()
    q_gain_t = jnp.concatenate([jnp.broadcast_to(gain[0:1, :], (HD, HD)).T] * (tb // HD), 1)

    first_block = 0
    for part, count in enumerate(parts):

        def normalise(b, carry, first_block=first_block, part=part):
            source = pl.ds(pl.multiple_of(b * tb, tb), tb)
            block = place[first_block + b]
            here = pl.ds(pl.multiple_of(block * tb, tb), tb)
            mine, other = projections[2 * part : 2 * part + 2]
            total = mine[source, :].astype(jnp.float32) + other[source, :].astype(jnp.float32)
            raw = total[:, :HD]
            inv = lax.rsqrt(jnp.mean(raw * raw, -1, keepdims=True) + EPS)
            qn[here, :] = (raw * inv * gain[0:1, :]).astype(jnp.bfloat16)
            raw_t = raw.T
            inv = lax.rsqrt(jnp.mean(raw_t * raw_t, 0, keepdims=True) + EPS)
            q_raw_t[block] = raw_t
            qn_t[block] = (raw_t * inv * q_gain_t).astype(jnp.bfloat16)
            raw = total[:, HD : 2 * HD]
            k_raw[here, :] = raw
            inv = lax.rsqrt(jnp.mean(raw * raw, -1, keepdims=True) + EPS)
            value = raw * inv * gain[1:2, :]
            kn[here, :] = value.astype(jnp.bfloat16)
            value_t = value.T.astype(jnp.bfloat16)
            for u in range(tb // HD):
                kn_t[block * (tb // HD) + u] = value_t[:, u * HD : (u + 1) * HD]
            vb[here, :] = total[:, 2 * HD :].astype(jnp.bfloat16)
            key_code[here, :] = jnp.broadcast_to(key_row[block], (HD, tb)).T
            return carry

        lax.fori_loop(0, count, normalise, 0)
        first_block += count
    for copy in cot_copies:
        copy.wait()

    def prepare(b, carry):
        here = pl.ds(pl.multiple_of(b * tb, tb), tb)
        do_t[b] = do[here, :].astype(jnp.float32).T.astype(jnp.bfloat16)
        dk[here, :] = jnp.zeros((tb, HD), jnp.float32)
        dv[here, :] = jnp.zeros((tb, HD), jnp.float32)
        return carry

    lax.fori_loop(0, nb, prepare, 0)

    def backward_norm(upstream, raw, weight, axis):
        inv = lax.rsqrt(jnp.mean(raw * raw, axis, keepdims=True) + EPS)
        weighted = weight * upstream
        cubed = inv * inv * inv
        return inv * weighted - raw * (cubed * jnp.mean(raw * weighted, axis, keepdims=True))

    def tile(start, length):
        here = pl.ds(pl.multiple_of(start, HD), length)
        offset = lax.broadcasted_iota(jnp.int32, (length, tb), 0) - lax.broadcasted_iota(
            jnp.int32, (length, tb), 1
        )
        return here, offset

    def forward(i, start, at, length, sums):
        here, offset = tile(start + at, length)
        s = jnp.dot(kn[here, :], qn_t[i], preferred_element_type=jnp.float32)
        codes = jnp.concatenate([key_code[here, :]] * (tb // HD), 1)
        allowed = (codes == clip_row[i]) | (offset == i * tb - start - at)
        e = jnp.where(allowed, jnp.exp2(s * (scale * math.log2(math.e))), 0.0)
        dp = jnp.dot(vb[here, :], do_t[i], preferred_element_type=jnp.float32)
        es[at : at + length, :] = e
        dps[at : at + length, :] = dp
        return (
            sums[0] + jnp.sum(e.reshape(length // 8, 8, tb), 0),
            sums[1] + jnp.sum((e * dp).reshape(length // 8, 8, tb), 0),
        )

    def finish_sums(sums):
        inv_l = 1.0 / jnp.sum(sums[0], 0, keepdims=True)
        return inv_l, jnp.sum(sums[1], 0, keepdims=True) * inv_l

    def backward(i, start, at, length, inv_l, row_dot, dq_t):
        here, _ = tile(start + at, length)
        rows_q = columns(i)
        p = es[at : at + length, :] * inv_l
        ds = (p * (dps[at : at + length, :] - row_dot)).astype(jnp.bfloat16)
        dv[here, :] += jnp.dot(
            p.astype(jnp.bfloat16), do[rows_q, :], preferred_element_type=jnp.float32
        )
        dk[here, :] += jnp.dot(ds, qn[rows_q, :], preferred_element_type=jnp.float32)
        first = (start + at) // HD
        for u in range(0, length, tb):
            keys_t = jnp.concatenate(
                [kn_t[first + (u + v) // HD] for v in range(0, min(tb, length - u), HD)], 1
            )
            dq_t += jnp.dot(keys_t, ds[u : u + tb], preferred_element_type=jnp.float32)
        return dq_t

    def columns(i):
        return pl.ds(pl.multiple_of(i * tb, tb), tb)

    def store_dq(i, dq_t):
        dproj_t[:HD, columns(i)] = backward_norm(dq_t * scale, q_raw_t[i], q_gain_t, 0).astype(
            jnp.bfloat16
        )

    zero = jnp.zeros((8, tb), jnp.float32)

    def query_block(i, start, lengths):
        sums = (zero, zero)
        at = 0
        for length in lengths:
            sums = forward(i, start, at, length, sums)
            at += length
        inv_l, row_dot = finish_sums(sums)
        dq_t = jnp.zeros((HD, tb), jnp.float32)
        at = 0
        for length in lengths:
            dq_t = backward(i, start, at, length, inv_l, row_dot, dq_t)
            at += length
        store_dq(i, dq_t)

    def queries(i, carry):
        inside = (place[nb + 3 * quarter + i] == windows[len(spans)]) & (
            place[2 * nb + 3 * quarter + i] == windows[len(spans)]
        )

        @pl.when(inside)
        def _():
            query_block(i, windows[0], cover(spans[0], 2 * tb))

        @pl.when(jnp.logical_not(inside))
        def _():
            query_block(i, 0, cover(nb * tb, 2 * tb))

        return carry

    lax.fori_loop(0, nb, queries, 0)

    def keys(b, carry):
        here = columns(b)
        value = backward_norm(dk[here, :] * scale, k_raw[here, :], gain[1:2, :], -1)
        dproj_t[HD : 2 * HD, here] = value.T.astype(jnp.bfloat16)
        dproj_t[2 * HD :, here] = dv[here, :].T.astype(jnp.bfloat16)
        return carry

    lax.fori_loop(0, nb, keys, 0)

    for copy in xcopies:
        copy.wait()
    for i, length in enumerate(spans):
        span = pl.ds(pl.multiple_of(windows[i], HD), length)
        mask = (clips[:, span] == windows[len(spans) + i]).astype(jnp.float32)
        part = jnp.dot(
            dproj_t[:, span] * mask.astype(jnp.bfloat16),
            xs[span, :],
            preferred_element_type=jnp.float32,
        )
        squares[...] = part * part if i == 0 else squares[...] + part * part
    running = jnp.zeros((3 * HD, rows), jnp.float32)
    for k in range(quarter):
        lanes = pl.ds(pl.multiple_of(place[nb + k] * rows, rows), rows)
        piece = squares[:, lanes]
        running += piece
        for j in range(3):
            fisher_out[k][j * rows : (j + 1) * rows, :] = (
                piece[j * HD : (j + 1) * HD, :].T.astype(jnp.bfloat16)
            )
    sum_out[...] = jnp.full((8, HD), jnp.sum(running), jnp.float32)


def finish_kernel(quarter, rows, shift, *refs):
    pieces = refs[:quarter]
    total, w, mask, ratio_out, damp_out = refs[quarter:]
    lane = pl.program_id(0)
    mean = total[0, 0] * (1.0 / (3 * D * HEADS * HD))
    factor = 1.0 / jnp.full((1, HD), mean + EPS, jnp.float32)
    damp = mask[...].astype(jnp.float32)
    for k in range(quarter):

        @pl.when(lax.rem(shift[0] + k, quarter) == lane)
        def _():
            for j in range(3):
                ratio = pieces[k][j * rows : (j + 1) * rows, :].astype(jnp.float32) * factor
                ratio_out[j] = ratio
                damp_out[j] = (w[j].astype(jnp.float32) / (1.0 + damp * ratio)).astype(
                    jnp.bfloat16
                )


def chip_per_head(tokens, w_qkv, gains, cotangent, token_clip, key_live, damp_mask, *, ns, nh):
    tb, width = tokens.shape
    rows, cols = w_qkv.shape[1:]
    quarter = cols // HD
    half = width // 2
    all_tokens = token_clip.shape[0]
    s = lax.axis_index("seq")
    h = lax.axis_index("head")
    core = h % 2
    vmem = pl.BlockSpec(memory_space=pltpu.VMEM)
    smem = pl.BlockSpec(memory_space=pltpu.SMEM)
    hbm = pl.BlockSpec(memory_space=pl.ANY)

    def index(si, hi):
        return si * nh + hi

    swap = [(index(a, b), index(a, b ^ 1)) for a in range(ns) for b in range(nh)]
    out_perms = []
    for k in range(quarter):
        out_perms.append(
            [
                (index(a, b), index((b % 2) * quarter + (k + a) % quarter, b - b % 2 + a // quarter))
                for a in range(ns)
                for b in range(nh)
            ]
        )
    back_perms = [[(b, a) for a, b in perm] for perm in out_perms]

    gains_other = lax.ppermute(gains, AXES, swap)
    outgoing = []
    for k in range(quarter):
        col = ((k + s) % quarter) * HD
        outgoing.append(
            jnp.concatenate(
                [
                    lax.dynamic_slice_in_dim(w_qkv, col, HD, 2).reshape(3 * rows, HD),
                    lax.dynamic_slice_in_dim(cotangent, col, HD, 1),
                ],
                0,
            )
        )
    pieces = []
    for k in range(0, quarter, 2):
        pair = outgoing[k : k + 2]
        if k:
            barred = lax.optimization_barrier((*pair, *pieces))
            pair, pieces = list(barred[: len(pair)]), list(barred[len(pair) :])
        pieces += [lax.ppermute(piece, AXES, out_perms[k + i]) for i, piece in enumerate(pair)]

    ring = list(range(0, ns, 2)) + list(range(1, ns, 2))[::-1]
    forth = [(ring[i], ring[(i + 1) % ns]) for i in range(ns)]
    back = [(b, a) for a, b in forth]
    position = [ring.index(i) for i in range(ns)]
    mine = lax.dynamic_slice_in_dim(tokens, core * half, half, 1)
    def halved(parts):
        return [half for part in parts for half in (part[: tb // 2], part[tb // 2 :])]

    ahead, behind = [mine], [mine]
    chunks, steps = [[mine]], [0]
    for step in range(1, ns // 2):
        if step == 3:
            ahead, behind = halved(ahead), halved(behind)
        ahead = [lax.ppermute(part, "seq", forth) for part in ahead]
        behind = [lax.ppermute(part, "seq", back) for part in behind]
        chunks += [ahead, behind]
        steps += [-step, step]
    chunks.append([lax.ppermute(ahead[0], "seq", forth), lax.ppermute(behind[1], "seq", back)])
    steps.append(ns // 2)
    blocks = token_clip.reshape(ns, tb)
    edges = (blocks[:, 0], blocks[:, -1])
    order = jnp.array([[ring[(position[i] + d) % ns] for d in steps] for i in range(ns)], jnp.int32)
    ks = jnp.arange(quarter, dtype=jnp.int32)
    row_block = ((s - ks) % quarter).astype(jnp.int32)
    place = jnp.concatenate(
        [
            lax.dynamic_index_in_dim(order, s, 0, False),
            row_block,
            row_block + core * quarter,
            row_block + (1 - core) * quarter,
            *edges,
        ]
    ).astype(jnp.int32)

    params = pltpu.CompilerParams(vmem_limit_bytes=VMEM_BYTES)
    bf16, f32 = jnp.bfloat16, jnp.float32
    own_gain = (s // quarter) == core
    gain = lax.dynamic_slice_in_dim(
        jnp.where(own_gain, gains, gains_other), (s % quarter) * HD, HD, 1
    )
    clip_row = token_clip.reshape(ns, 1, tb)
    key_row = jnp.where(key_live == 1, token_clip, -1).reshape(ns, 1, tb)
    clip_ids = jnp.arange(CLIPS, dtype=jnp.int32)
    starts = jnp.sum(token_clip[None] < clip_ids[:, None], 1, dtype=jnp.int32)
    sizes = jnp.sum(token_clip[None] == clip_ids[:, None], 1, dtype=jnp.int32)
    longest = jnp.argmax(sizes).astype(jnp.int32)
    ordered = jnp.stack([longest] + [(longest + i) % CLIPS for i in range(1, CLIPS)])
    spans = (3 * all_tokens // 4 + HD,) + (all_tokens // 4 + HD,) * (CLIPS - 1)
    windows = jnp.minimum(starts[ordered] // HD * HD, all_tokens - jnp.array(spans, jnp.int32))
    windows = jnp.concatenate([windows, ordered]).astype(jnp.int32)
    place, row_block, windows, gain, clip_row, key_row, *pieces = lax.optimization_barrier(
        (place, row_block, windows, gain, clip_row, key_row, *pieces)
    )
    layout = []
    for block, group in enumerate(chunks):
        offset = 0
        for part in group:
            layout.append((block, offset, part.shape[0]))
            offset += part.shape[0]
    parts = (ns - 3, 3)
    projections = []
    at = 0
    for part, count in enumerate(parts):
        group = [array for block in chunks[at : at + count] for array in block]
        partial, *cot = project(group, pieces, row_block, tb, part == 0)
        projections += [partial, lax.ppermute(partial, AXES, swap)]
        at += count
        if part == 0:
            cot_mine = cot[0]
            cot_other = lax.ppermute(cot_mine, AXES, swap)
    arrays = [array for block in chunks for array in block]
    *fisher, part_sum = pl.pallas_call(
        functools.partial(head_kernel, ns, tb, rows, quarter, parts, tuple(layout), spans),
        out_shape=(
            *[jax.ShapeDtypeStruct((3 * rows, HD), bf16)] * quarter,
            jax.ShapeDtypeStruct((8, HD), f32),
        ),
        in_specs=[smem, smem] + [hbm] * (len(arrays) + 2) + [vmem] * (len(projections) + 4),
        out_specs=[vmem] * (quarter + 1),
        scratch_shapes=[
            pltpu.VMEM((all_tokens, HD), bf16),
            pltpu.VMEM((ns, HD, tb), f32),
            pltpu.VMEM((all_tokens, HD), f32),
            pltpu.VMEM((all_tokens, HD), bf16),
            pltpu.VMEM((all_tokens, HD), bf16),
            pltpu.VMEM((all_tokens, HD), bf16),
            pltpu.VMEM((ns, HD, tb), bf16),
            pltpu.VMEM((all_tokens // HD, HD, HD), bf16),
            pltpu.VMEM((ns, HD, tb), bf16),
            pltpu.VMEM((all_tokens, HD), jnp.int32),
            pltpu.VMEM((all_tokens, tb), f32),
            pltpu.VMEM((all_tokens, tb), f32),
            pltpu.VMEM((all_tokens, HD), f32),
            pltpu.VMEM((all_tokens, HD), f32),
            pltpu.VMEM((3 * HD, all_tokens), bf16),
            pltpu.VMEM((all_tokens, half), bf16),
            pltpu.VMEM((3 * HD, half), f32),
            pltpu.SemaphoreType.DMA((len(arrays),)),
            pltpu.SemaphoreType.DMA((2, quarter)),
        ],
        compiler_params=params,
        cost_estimate=pl.CostEstimate(flops=34100000000, bytes_accessed=111600000, transcendentals=0),
        name="head",
    )(
        place,
        windows,
        *arrays,
        cot_mine,
        cot_other,
        *projections,
        gain,
        clip_row,
        key_row,
        token_clip[None],
    )

    returned = [lax.ppermute(fisher[k], AXES, back_perms[k]) for k in range(quarter)]
    total = part_sum[:1]
    bit = 1
    while bit < nh:
        total = total + lax.ppermute(total, "head", [(i, i ^ bit) for i in range(nh)])
        bit *= 2
    bit = 1
    while bit < ns:
        total = total + lax.ppermute(total, "seq", [(i, i ^ bit) for i in range(ns)])
        bit *= 2
    shift = (s % quarter).astype(jnp.int32).reshape(1)
    full = lambda i, shift: (0, 0)
    lanes = lambda i, shift: (0, 0, i)
    return pl.pallas_call(
        functools.partial(finish_kernel, quarter, rows),
        out_shape=(
            jax.ShapeDtypeStruct((3, rows, cols), f32),
            jax.ShapeDtypeStruct((3, rows, cols), bf16),
        ),
        grid_spec=pltpu.PrefetchScalarGridSpec(
            num_scalar_prefetch=1,
            grid=(quarter,),
            in_specs=[pl.BlockSpec((3 * rows, HD), full)] * quarter
            + [
                pl.BlockSpec((1, HD), full, memory_space=pltpu.SMEM),
                pl.BlockSpec((3, rows, HD), lanes),
                pl.BlockSpec((rows, HD), lambda i, shift: (0, i)),
            ],
            out_specs=(
                pl.BlockSpec((3, rows, HD), lanes),
                pl.BlockSpec((3, rows, HD), lanes),
            ),
        ),
        compiler_params=params,
        cost_estimate=pl.CostEstimate(flops=5500000000, bytes_accessed=18000000, transcendentals=0),
        name="finish",
    )(shift, *returned, total, w_qkv, damp_mask)


def solution(mesh):
    ns, nh = mesh.shape["seq"], mesh.shape["head"]

    def on_device(*args):
        if ns == 2 * (args[1].shape[2] // HD) and ns & (ns - 1) == 0 and nh % 2 == 0 and args[4].shape[0] % (4 * HD) == 0:
            return chip_per_head(*args, ns=ns, nh=nh)
        return row_sharded(*args)

    return jax.shard_map(
        on_device,
        mesh=mesh,
        in_specs=(
            P("seq", None),
            P(None, "seq", "head"),
            P(None, "head"),
            P("seq", "head"),
            P(),
            P(),
            P("seq", "head"),
        ),
        out_specs=(P(None, "seq", "head"), P(None, "seq", "head")),
        check_vma=False,
    )
```

```python
import functools
import math

import jax
import jax.numpy as jnp
from jax import lax
from jax.experimental import pallas as pl
from jax.experimental.pallas import tpu as pltpu
from jax.sharding import PartitionSpec as P

D = 3072
HD = 128
HEADS = 16
CLIPS = 3
EPS = 1e-6
VMEM_BYTES = 56 * 1024 * 1024
AXES = ("seq", "head")


def normed(values, gain_row, head_count):
    shaped = values.reshape(values.shape[0], head_count, HD)
    inverse = lax.rsqrt(jnp.mean(shaped * shaped, -1, keepdims=True) + EPS)
    return (shaped * inverse * gain_row.reshape(head_count, HD), inverse, shaped)


def unnorm(upstream, shaped, inverse, gain_row, head_count):
    gain_grid = gain_row.reshape(head_count, HD)
    cubed = inverse * inverse * inverse
    return inverse * gain_grid * upstream - shaped * cubed * jnp.mean(
        shaped * gain_grid * upstream, -1, keepdims=True
    )


def by_clip(grad_rows, clip_ids):
    return jnp.concatenate(
        [
            grad_rows * (clip_ids == clip_no).astype(jnp.bfloat16)[..., None]
            for clip_no in range(CLIPS)
        ],
        -1,
    )


def row_sharded(tokens, w_qkv, gains, cotangent, token_clip, key_live, damp_mask):
    tok_rows = tokens.shape[0]
    width_dev = w_qkv.shape[2]
    rows_dev = w_qkv.shape[1]
    head_count = width_dev // HD
    all_tokens = token_clip.shape[0]
    seq_rank = lax.axis_index("seq")
    score_scale = 1.0 / math.sqrt(HD)
    projected = jnp.einsum(
        "tr,jrc->jtc",
        tokens,
        lax.all_gather(w_qkv, "seq", axis=1, tiled=True),
        preferred_element_type=jnp.float32,
    )
    query_n, query_inv, query_raw = normed(projected[0], gains[0], head_count)
    key_n, key_inv, key_raw = normed(projected[1], gains[1], head_count)
    query_b = query_n.astype(jnp.bfloat16)
    local_kv = jnp.concatenate(
        [
            key_n.astype(jnp.bfloat16).reshape(tok_rows, width_dev),
            projected[2].astype(jnp.bfloat16),
        ],
        1,
    )
    all_kv = lax.all_gather(local_kv, "seq", axis=0, tiled=True)
    keys_all = all_kv[:, :width_dev].reshape(all_tokens, head_count, HD)
    values_all = all_kv[:, width_dev:].reshape(all_tokens, head_count, HD)
    first_row = seq_rank * tok_rows
    clip_here = lax.dynamic_slice_in_dim(token_clip, first_row, tok_rows)
    positions = first_row + jnp.arange(tok_rows, dtype=jnp.int32)
    key_positions = jnp.arange(all_tokens, dtype=jnp.int32)
    allowed = (clip_here[:, None] == token_clip[None, :]) & (
        (key_live[None, :] == 1) | (positions[:, None] == key_positions[None, :])
    )
    scores = (
        jnp.einsum("thd,khd->htk", query_b, keys_all, preferred_element_type=jnp.float32)
        * score_scale
    )
    scores = jnp.where(allowed[None], scores, -1e30)
    peak = jnp.max(scores, -1, keepdims=True)
    expd = jnp.exp(scores - peak)
    probs = expd / jnp.sum(expd, -1, keepdims=True)
    grad_out = cotangent.reshape(tok_rows, head_count, HD)
    grad_p = jnp.einsum("thd,khd->htk", grad_out, values_all, preferred_element_type=jnp.float32)
    row_dot = jnp.sum(probs * grad_p, -1, keepdims=True)
    ds_half = (probs * (grad_p - row_dot)).astype(jnp.bfloat16)
    probs_half = probs.astype(jnp.bfloat16)
    grad_qn = (
        jnp.einsum("htk,khd->thd", ds_half, keys_all, preferred_element_type=jnp.float32)
        * score_scale
    )
    key_part = (
        jnp.einsum("htk,thd->khd", ds_half, query_b, preferred_element_type=jnp.float32)
        * score_scale
    )
    value_part = jnp.einsum(
        "htk,thd->khd", probs_half, grad_out, preferred_element_type=jnp.float32
    )
    key_terms = jnp.concatenate(
        [key_part.reshape(all_tokens, width_dev), value_part.reshape(all_tokens, width_dev)], 1
    )
    summed = lax.psum_scatter(
        key_terms.astype(jnp.bfloat16), "seq", scatter_dimension=0, tiled=True
    ).astype(jnp.float32)
    grad_q = unnorm(grad_qn, query_raw, query_inv, gains[0], head_count)
    grad_k = unnorm(
        summed[:, :width_dev].reshape(tok_rows, head_count, HD),
        key_raw,
        key_inv,
        gains[1],
        head_count,
    )
    grad_proj = jnp.concatenate(
        [
            grad_q.reshape(tok_rows, width_dev),
            grad_k.reshape(tok_rows, width_dev),
            summed[:, width_dev:],
        ],
        1,
    ).astype(jnp.bfloat16)
    masked = by_clip(grad_proj, clip_here)
    per_clip = lax.psum_scatter(
        lax.dot_general(
            tokens, masked, (((0,), (0,)), ((), ())), preferred_element_type=jnp.float32
        ).astype(jnp.bfloat16),
        "seq",
        scatter_dimension=0,
        tiled=True,
    ).astype(jnp.float32)
    fisher = jnp.sum(jnp.square(per_clip.reshape(rows_dev, CLIPS, 3, width_dev)), 1)
    fisher = jnp.transpose(fisher, (1, 0, 2))
    fisher_sum = lax.psum(jnp.sum(fisher), AXES)
    fisher_mean = fisher_sum / (3 * D * HEADS * HD)
    fisher_ratio = fisher / (fisher_mean + EPS)
    dampened = (
        w_qkv.astype(jnp.float32) / (1.0 + damp_mask.astype(jnp.float32)[None] * fisher_ratio)
    ).astype(jnp.bfloat16)
    return (fisher_ratio, dampened)


def project_kernel(nb, tb, rows, quarter, with_cot, place, *refs):
    chunks = refs[:nb]
    pieces = refs[nb : nb + quarter]
    outs = refs[nb + quarter : -6]
    xs, ws, cs, xsem, wsem, csem = refs[-6:]
    copies = []
    for k in range(quarter):
        start = pl.multiple_of(place[k] * rows, rows)
        for j in range(3):
            copies.append(
                pltpu.make_async_copy(
                    pieces[k].at[pl.ds(j * rows, rows)],
                    ws.at[pl.ds(start, rows), pl.ds(j * HD, HD)],
                    wsem.at[k, j],
                )
            )
        if with_cot:
            copies.append(
                pltpu.make_async_copy(
                    pieces[k].at[pl.ds(3 * rows, tb)], cs.at[pl.ds(k * tb, tb)], csem.at[k]
                )
            )
    xcopies = []
    at = 0
    for b, chunk in enumerate(chunks):
        height = chunk.shape[0]
        xcopies.append(pltpu.make_async_copy(chunk, xs.at[pl.ds(at, height)], xsem.at[b]))
        at += height
    for copy in copies + xcopies:
        copy.start()
    for copy in copies:
        copy.wait()
    if with_cot:
        outs[1][...] = cs[...]
    for copy in xcopies:
        copy.wait()
    part = jnp.dot(xs[...], ws[...], preferred_element_type=jnp.float32)
    outs[0][...] = part.astype(jnp.bfloat16)


def project(chunks, pieces, row_block, tb, with_cot):
    nb, quarter = len(chunks), len(pieces)
    half = chunks[0].shape[1]
    total = sum(chunk.shape[0] for chunk in chunks)
    rows = (pieces[0].shape[0] - tb) // 3
    vmem = pl.BlockSpec(memory_space=pltpu.VMEM)
    shapes = [
        jax.ShapeDtypeStruct((total, 3 * HD), jnp.bfloat16),
    ]
    if with_cot:
        shapes.append(jax.ShapeDtypeStruct((quarter * tb, HD), jnp.bfloat16))
    return pl.pallas_call(
        functools.partial(project_kernel, nb, tb, rows, quarter, with_cot),
        out_shape=shapes,
        in_specs=[pl.BlockSpec(memory_space=pltpu.SMEM)]
        + [pl.BlockSpec(memory_space=pl.ANY)] * (nb + quarter),
        out_specs=[vmem] * len(shapes),
        scratch_shapes=[
            pltpu.VMEM((total, half), jnp.bfloat16),
            pltpu.VMEM((half, 3 * HD), jnp.bfloat16),
            pltpu.VMEM((quarter * tb, HD), jnp.bfloat16),
            pltpu.SemaphoreType.DMA((nb,)),
            pltpu.SemaphoreType.DMA((quarter, 3)),
            pltpu.SemaphoreType.DMA((quarter,)),
        ],
        compiler_params=pltpu.CompilerParams(vmem_limit_bytes=VMEM_BYTES),
        cost_estimate=pl.CostEstimate(flops=8800000000, bytes_accessed=28800000, transcendentals=0),
        name="project",
    )(row_block, *chunks, *pieces)


def cover(total, unit):
    count = max(1, total // unit)
    return (unit,) * (count - 1) + (total - unit * (count - 1),)


def head_kernel(nb, tb, rows, quarter, parts, layout, spans, place, windows, *refs):
    nc = len(layout)
    chunks = refs[:nc]
    cots = refs[nc : nc + 2]
    ends = nc + 2 + 2 * len(parts)
    projections = refs[nc + 2 : ends]
    gain, clip_row, key_row, clips = refs[ends : ends + 4]
    fisher_out = refs[ends + 4 : ends + 4 + quarter]
    sum_out = refs[ends + 4 + quarter]
    (do, q_raw_t, k_raw, qn, kn, vb, qn_t, kn_t, do_t, key_code, es, dps, dk, dv) = refs[
        ends + 5 + quarter : -5
    ]
    dproj_t, xs, squares, xsem, csem = refs[-5:]
    scale = 1.0 / math.sqrt(HD)
    cot_copies = []
    for k in range(quarter):
        for side in range(2):
            src = cots[side].at[pl.ds(k * tb, tb)]
            block = place[nb + quarter * (1 + side) + k]
            cot_copies.append(
                pltpu.make_async_copy(
                    src, do.at[pl.ds(pl.multiple_of(block * tb, tb), tb)], csem.at[side, k]
                )
            )
    xcopies = []
    for b, (block, offset, count) in enumerate(layout):
        start = pl.multiple_of(place[block] * tb + offset, count)
        xcopies.append(pltpu.make_async_copy(chunks[b], xs.at[pl.ds(start, count)], xsem.at[b]))
    for copy in cot_copies + xcopies:
        copy.start()
    q_gain_t = jnp.concatenate([jnp.broadcast_to(gain[0:1, :], (HD, HD)).T] * (tb // HD), 1)

    first_block = 0
    for part, count in enumerate(parts):

        def normalise(b, carry, first_block=first_block, part=part):
            source = pl.ds(pl.multiple_of(b * tb, tb), tb)
            block = place[first_block + b]
            here = pl.ds(pl.multiple_of(block * tb, tb), tb)
            mine, other = projections[2 * part : 2 * part + 2]
            total = mine[source, :].astype(jnp.float32) + other[source, :].astype(jnp.float32)
            raw = total[:, :HD]
            inv = lax.rsqrt(jnp.mean(raw * raw, -1, keepdims=True) + EPS)
            qn[here, :] = (raw * inv * gain[0:1, :]).astype(jnp.bfloat16)
            raw_t = raw.T
            inv = lax.rsqrt(jnp.mean(raw_t * raw_t, 0, keepdims=True) + EPS)
            q_raw_t[block] = raw_t
            qn_t[block] = (raw_t * inv * q_gain_t).astype(jnp.bfloat16)
            raw = total[:, HD : 2 * HD]
            k_raw[here, :] = raw
            inv = lax.rsqrt(jnp.mean(raw * raw, -1, keepdims=True) + EPS)
            value = raw * inv * gain[1:2, :]
            kn[here, :] = value.astype(jnp.bfloat16)
            value_t = value.T.astype(jnp.bfloat16)
            for u in range(tb // HD):
                kn_t[block * (tb // HD) + u] = value_t[:, u * HD : (u + 1) * HD]
            vb[here, :] = total[:, 2 * HD :].astype(jnp.bfloat16)
            key_code[here, :] = jnp.broadcast_to(key_row[block], (HD, tb)).T
            return carry

        lax.fori_loop(0, count, normalise, 0)
        first_block += count
    for copy in cot_copies:
        copy.wait()

    def prepare(b, carry):
        here = pl.ds(pl.multiple_of(b * tb, tb), tb)
        do_t[b] = do[here, :].astype(jnp.float32).T.astype(jnp.bfloat16)
        dk[here, :] = jnp.zeros((tb, HD), jnp.float32)
        dv[here, :] = jnp.zeros((tb, HD), jnp.float32)
        return carry

    lax.fori_loop(0, nb, prepare, 0)

    def backward_norm(upstream, raw, weight, axis):
        inv = lax.rsqrt(jnp.mean(raw * raw, axis, keepdims=True) + EPS)
        weighted = weight * upstream
        cubed = inv * inv * inv
        return inv * weighted - raw * (cubed * jnp.mean(raw * weighted, axis, keepdims=True))

    def tile(start, length):
        here = pl.ds(pl.multiple_of(start, HD), length)
        offset = lax.broadcasted_iota(jnp.int32, (length, tb), 0) - lax.broadcasted_iota(
            jnp.int32, (length, tb), 1
        )
        return here, offset

    def forward(i, start, at, length, sums):
        here, offset = tile(start + at, length)
        s = jnp.dot(kn[here, :], qn_t[i], preferred_element_type=jnp.float32)
        codes = jnp.concatenate([key_code[here, :]] * (tb // HD), 1)
        allowed = (codes == clip_row[i]) | (offset == i * tb - start - at)
        e = jnp.where(allowed, jnp.exp2(s * (scale * math.log2(math.e))), 0.0)
        dp = jnp.dot(vb[here, :], do_t[i], preferred_element_type=jnp.float32)
        es[at : at + length, :] = e
        dps[at : at + length, :] = dp
        return (
            sums[0] + jnp.sum(e.reshape(length // 8, 8, tb), 0),
            sums[1] + jnp.sum((e * dp).reshape(length // 8, 8, tb), 0),
        )

    def finish_sums(sums):
        inv_l = 1.0 / jnp.sum(sums[0], 0, keepdims=True)
        return inv_l, jnp.sum(sums[1], 0, keepdims=True) * inv_l

    def backward(i, start, at, length, inv_l, row_dot, dq_t):
        here, _ = tile(start + at, length)
        rows_q = columns(i)
        p = es[at : at + length, :] * inv_l
        ds = (p * (dps[at : at + length, :] - row_dot)).astype(jnp.bfloat16)
        dv[here, :] += jnp.dot(
            p.astype(jnp.bfloat16), do[rows_q, :], preferred_element_type=jnp.float32
        )
        dk[here, :] += jnp.dot(ds, qn[rows_q, :], preferred_element_type=jnp.float32)
        first = (start + at) // HD
        for u in range(0, length, tb):
            keys_t = jnp.concatenate(
                [kn_t[first + (u + v) // HD] for v in range(0, min(tb, length - u), HD)], 1
            )
            dq_t += jnp.dot(keys_t, ds[u : u + tb], preferred_element_type=jnp.float32)
        return dq_t

    def columns(i):
        return pl.ds(pl.multiple_of(i * tb, tb), tb)

    def store_dq(i, dq_t):
        dproj_t[:HD, columns(i)] = backward_norm(dq_t * scale, q_raw_t[i], q_gain_t, 0).astype(
            jnp.bfloat16
        )

    zero = jnp.zeros((8, tb), jnp.float32)

    def query_block(i, start, lengths):
        sums = (zero, zero)
        at = 0
        for length in lengths:
            sums = forward(i, start, at, length, sums)
            at += length
        inv_l, row_dot = finish_sums(sums)
        dq_t = jnp.zeros((HD, tb), jnp.float32)
        at = 0
        for length in lengths:
            dq_t = backward(i, start, at, length, inv_l, row_dot, dq_t)
            at += length
        store_dq(i, dq_t)

    def queries(i, carry):
        inside = (place[nb + 3 * quarter + i] == windows[len(spans)]) & (
            place[2 * nb + 3 * quarter + i] == windows[len(spans)]
        )

        @pl.when(inside)
        def _():
            query_block(i, windows[0], cover(spans[0], 2 * tb))

        @pl.when(jnp.logical_not(inside))
        def _():
            query_block(i, 0, cover(nb * tb, 2 * tb))

        return carry

    lax.fori_loop(0, nb, queries, 0)

    def keys(b, carry):
        here = columns(b)
        value = backward_norm(dk[here, :] * scale, k_raw[here, :], gain[1:2, :], -1)
        dproj_t[HD : 2 * HD, here] = value.T.astype(jnp.bfloat16)
        dproj_t[2 * HD :, here] = dv[here, :].T.astype(jnp.bfloat16)
        return carry

    lax.fori_loop(0, nb, keys, 0)

    for copy in xcopies:
        copy.wait()
    for i, length in enumerate(spans):
        span = pl.ds(pl.multiple_of(windows[i], HD), length)
        mask = (clips[:, span] == windows[len(spans) + i]).astype(jnp.float32)
        part = jnp.dot(
            dproj_t[:, span] * mask.astype(jnp.bfloat16),
            xs[span, :],
            preferred_element_type=jnp.float32,
        )
        squares[...] = part * part if i == 0 else squares[...] + part * part
    running = jnp.zeros((3 * HD, rows), jnp.float32)
    for k in range(quarter):
        lanes = pl.ds(pl.multiple_of(place[nb + k] * rows, rows), rows)
        piece = squares[:, lanes]
        running += piece
        for j in range(3):
            fisher_out[k][j * rows : (j + 1) * rows, :] = (
                piece[j * HD : (j + 1) * HD, :].T.astype(jnp.bfloat16)
            )
    sum_out[...] = jnp.full((8, HD), jnp.sum(running), jnp.float32)


def finish_kernel(quarter, rows, shift, total, w, mask, *refs):
    pieces = refs[:quarter]
    ratio_out, damp_out, w_in, mask_in, ratio_buf, damp_buf, in_sem, out_sem = refs[quarter:]
    loads, stores = [], []
    for k in range(quarter):
        lanes = pl.ds(pl.multiple_of(lax.rem(shift[0] + k, quarter) * HD, HD), HD)
        loads.append(
            (
                pltpu.make_async_copy(w.at[:, :, lanes], w_in.at[k], in_sem.at[0, k]),
                pltpu.make_async_copy(mask.at[:, lanes], mask_in.at[k], in_sem.at[1, k]),
            )
        )
        stores.append(
            (
                pltpu.make_async_copy(ratio_buf.at[k], ratio_out.at[:, :, lanes], out_sem.at[0, k]),
                pltpu.make_async_copy(damp_buf.at[k], damp_out.at[:, :, lanes], out_sem.at[1, k]),
            )
        )
    for pair in loads:
        for copy in pair:
            copy.start()
    mean = total[0, 0] * (1.0 / (3 * D * HEADS * HD))
    factor = 1.0 / jnp.full((1, HD), mean + EPS, jnp.float32)
    for k in range(quarter):
        for copy in loads[k]:
            copy.wait()
        damp = mask_in[k].astype(jnp.float32)
        for j in range(3):
            ratio = pieces[k][j * rows : (j + 1) * rows, :].astype(jnp.float32) * factor
            ratio_buf[k, j] = ratio
            damp_buf[k, j] = (w_in[k, j].astype(jnp.float32) / (1.0 + damp * ratio)).astype(
                jnp.bfloat16
            )
        for copy in stores[k]:
            copy.start()
    for pair in stores:
        for copy in pair:
            copy.wait()


def chip_per_head(tokens, w_qkv, gains, cotangent, token_clip, key_live, damp_mask, *, ns, nh):
    tb, width = tokens.shape
    rows, cols = w_qkv.shape[1:]
    quarter = cols // HD
    half = width // 2
    all_tokens = token_clip.shape[0]
    s = lax.axis_index("seq")
    h = lax.axis_index("head")
    core = h % 2
    vmem = pl.BlockSpec(memory_space=pltpu.VMEM)
    smem = pl.BlockSpec(memory_space=pltpu.SMEM)
    hbm = pl.BlockSpec(memory_space=pl.ANY)

    def index(si, hi):
        return si * nh + hi

    swap = [(index(a, b), index(a, b ^ 1)) for a in range(ns) for b in range(nh)]
    out_perms = []
    for k in range(quarter):
        out_perms.append(
            [
                (index(a, b), index((b % 2) * quarter + (k + a) % quarter, b - b % 2 + a // quarter))
                for a in range(ns)
                for b in range(nh)
            ]
        )
    back_perms = [[(b, a) for a, b in perm] for perm in out_perms]

    gains_other = lax.ppermute(gains, AXES, swap)
    outgoing = []
    for k in range(quarter):
        col = ((k + s) % quarter) * HD
        outgoing.append(
            jnp.concatenate(
                [
                    lax.dynamic_slice_in_dim(w_qkv, col, HD, 2).reshape(3 * rows, HD),
                    lax.dynamic_slice_in_dim(cotangent, col, HD, 1),
                ],
                0,
            )
        )
    pieces = []
    for k in range(0, quarter, 2):
        pair = outgoing[k : k + 2]
        if k:
            barred = lax.optimization_barrier((*pair, *pieces))
            pair, pieces = list(barred[: len(pair)]), list(barred[len(pair) :])
        pieces += [lax.ppermute(piece, AXES, out_perms[k + i]) for i, piece in enumerate(pair)]

    ring = list(range(0, ns, 2)) + list(range(1, ns, 2))[::-1]
    forth = [(ring[i], ring[(i + 1) % ns]) for i in range(ns)]
    back = [(b, a) for a, b in forth]
    position = [ring.index(i) for i in range(ns)]
    mine = lax.dynamic_slice_in_dim(tokens, core * half, half, 1)
    def halved(parts):
        return [half for part in parts for half in (part[: tb // 2], part[tb // 2 :])]

    ahead, behind = [mine], [mine]
    chunks, steps = [[mine]], [0]
    for step in range(1, ns // 2):
        if step == 3:
            ahead, behind = halved(ahead), halved(behind)
        ahead = [lax.ppermute(part, "seq", forth) for part in ahead]
        behind = [lax.ppermute(part, "seq", back) for part in behind]
        chunks += [ahead, behind]
        steps += [-step, step]
    chunks.append([lax.ppermute(ahead[0], "seq", forth), lax.ppermute(behind[1], "seq", back)])
    steps.append(ns // 2)
    blocks = token_clip.reshape(ns, tb)
    edges = (blocks[:, 0], blocks[:, -1])
    order = jnp.array([[ring[(position[i] + d) % ns] for d in steps] for i in range(ns)], jnp.int32)
    ks = jnp.arange(quarter, dtype=jnp.int32)
    row_block = ((s - ks) % quarter).astype(jnp.int32)
    place = jnp.concatenate(
        [
            lax.dynamic_index_in_dim(order, s, 0, False),
            row_block,
            row_block + core * quarter,
            row_block + (1 - core) * quarter,
            *edges,
        ]
    ).astype(jnp.int32)

    params = pltpu.CompilerParams(vmem_limit_bytes=VMEM_BYTES)
    bf16, f32 = jnp.bfloat16, jnp.float32
    own_gain = (s // quarter) == core
    gain = lax.dynamic_slice_in_dim(
        jnp.where(own_gain, gains, gains_other), (s % quarter) * HD, HD, 1
    )
    clip_row = token_clip.reshape(ns, 1, tb)
    key_row = jnp.where(key_live == 1, token_clip, -1).reshape(ns, 1, tb)
    clip_ids = jnp.arange(CLIPS, dtype=jnp.int32)
    starts = jnp.sum(token_clip[None] < clip_ids[:, None], 1, dtype=jnp.int32)
    sizes = jnp.sum(token_clip[None] == clip_ids[:, None], 1, dtype=jnp.int32)
    longest = jnp.argmax(sizes).astype(jnp.int32)
    ordered = jnp.stack([longest] + [(longest + i) % CLIPS for i in range(1, CLIPS)])
    spans = (3 * all_tokens // 4 + HD,) + (all_tokens // 4 + HD,) * (CLIPS - 1)
    windows = jnp.minimum(starts[ordered] // HD * HD, all_tokens - jnp.array(spans, jnp.int32))
    windows = jnp.concatenate([windows, ordered]).astype(jnp.int32)
    place, row_block, windows, gain, clip_row, key_row, *pieces = lax.optimization_barrier(
        (place, row_block, windows, gain, clip_row, key_row, *pieces)
    )
    layout = []
    for block, group in enumerate(chunks):
        offset = 0
        for part in group:
            layout.append((block, offset, part.shape[0]))
            offset += part.shape[0]
    parts = (ns - 3, 3)
    projections = []
    at = 0
    for part, count in enumerate(parts):
        group = [array for block in chunks[at : at + count] for array in block]
        partial, *cot = project(group, pieces, row_block, tb, part == 0)
        projections += [partial, lax.ppermute(partial, AXES, swap)]
        at += count
        if part == 0:
            cot_mine = cot[0]
            cot_other = lax.ppermute(cot_mine, AXES, swap)
    arrays = [array for block in chunks for array in block]
    *fisher, part_sum = pl.pallas_call(
        functools.partial(head_kernel, ns, tb, rows, quarter, parts, tuple(layout), spans),
        out_shape=(
            *[jax.ShapeDtypeStruct((3 * rows, HD), bf16)] * quarter,
            jax.ShapeDtypeStruct((8, HD), f32),
        ),
        in_specs=[smem, smem] + [hbm] * (len(arrays) + 2) + [vmem] * (len(projections) + 4),
        out_specs=[vmem] * (quarter + 1),
        scratch_shapes=[
            pltpu.VMEM((all_tokens, HD), bf16),
            pltpu.VMEM((ns, HD, tb), f32),
            pltpu.VMEM((all_tokens, HD), f32),
            pltpu.VMEM((all_tokens, HD), bf16),
            pltpu.VMEM((all_tokens, HD), bf16),
            pltpu.VMEM((all_tokens, HD), bf16),
            pltpu.VMEM((ns, HD, tb), bf16),
            pltpu.VMEM((all_tokens // HD, HD, HD), bf16),
            pltpu.VMEM((ns, HD, tb), bf16),
            pltpu.VMEM((all_tokens, HD), jnp.int32),
            pltpu.VMEM((all_tokens, tb), f32),
            pltpu.VMEM((all_tokens, tb), f32),
            pltpu.VMEM((all_tokens, HD), f32),
            pltpu.VMEM((all_tokens, HD), f32),
            pltpu.VMEM((3 * HD, all_tokens), bf16),
            pltpu.VMEM((all_tokens, half), bf16),
            pltpu.VMEM((3 * HD, half), f32),
            pltpu.SemaphoreType.DMA((len(arrays),)),
            pltpu.SemaphoreType.DMA((2, quarter)),
        ],
        compiler_params=params,
        cost_estimate=pl.CostEstimate(flops=34100000000, bytes_accessed=111600000, transcendentals=0),
        name="head",
    )(
        place,
        windows,
        *arrays,
        cot_mine,
        cot_other,
        *projections,
        gain,
        clip_row,
        key_row,
        token_clip[None],
    )

    returned = [lax.ppermute(fisher[k], AXES, back_perms[k]) for k in range(quarter)]
    total = part_sum[:1]
    bit = 1
    while bit < nh:
        total = total + lax.ppermute(total, "head", [(i, i ^ bit) for i in range(nh)])
        bit *= 2
    bit = 1
    while bit < ns:
        total = total + lax.ppermute(total, "seq", [(i, i ^ bit) for i in range(ns)])
        bit *= 2
    shift = (s % quarter).astype(jnp.int32).reshape(1)
    hbm_only = pl.BlockSpec(memory_space=pltpu.HBM)
    return pl.pallas_call(
        functools.partial(finish_kernel, quarter, rows),
        out_shape=(
            jax.ShapeDtypeStruct((3, rows, cols), f32),
            jax.ShapeDtypeStruct((3, rows, cols), bf16),
        ),
        in_specs=[smem, smem, hbm_only, hbm_only] + [vmem] * quarter,
        out_specs=[hbm_only] * 2,
        scratch_shapes=[
            pltpu.VMEM((quarter, 3, rows, HD), bf16),
            pltpu.VMEM((quarter, rows, HD), jnp.int32),
            pltpu.VMEM((quarter, 3, rows, HD), f32),
            pltpu.VMEM((quarter, 3, rows, HD), bf16),
            pltpu.SemaphoreType.DMA((2, quarter)),
            pltpu.SemaphoreType.DMA((2, quarter)),
        ],
        compiler_params=params,
        cost_estimate=pl.CostEstimate(flops=5500000000, bytes_accessed=18000000, transcendentals=0),
        name="finish",
    )(shift, total, w_qkv, damp_mask, *returned)


def solution(mesh):
    ns, nh = mesh.shape["seq"], mesh.shape["head"]

    def on_device(*args):
        if ns == 2 * (args[1].shape[2] // HD) and ns & (ns - 1) == 0 and nh % 2 == 0 and args[4].shape[0] % (4 * HD) == 0:
            return chip_per_head(*args, ns=ns, nh=nh)
        return row_sharded(*args)

    return jax.shard_map(
        on_device,
        mesh=mesh,
        in_specs=(
            P("seq", None),
            P(None, "seq", "head"),
            P(None, "head"),
            P("seq", "head"),
            P(),
            P(),
            P("seq", "head"),
        ),
        out_specs=(P(None, "seq", "head"), P(None, "seq", "head")),
        check_vma=False,
    )
```

```python
import functools
import math

import jax
import jax.numpy as jnp
from jax import lax
from jax.experimental import pallas as pl
from jax.experimental.pallas import tpu as pltpu
from jax.sharding import PartitionSpec as P

D = 3072
HD = 128
HEADS = 16
CLIPS = 3
EPS = 1e-6
VMEM_BYTES = 56 * 1024 * 1024
AXES = ("seq", "head")


def normed(values, gain_row, head_count):
    shaped = values.reshape(values.shape[0], head_count, HD)
    inverse = lax.rsqrt(jnp.mean(shaped * shaped, -1, keepdims=True) + EPS)
    return (shaped * inverse * gain_row.reshape(head_count, HD), inverse, shaped)


def unnorm(upstream, shaped, inverse, gain_row, head_count):
    gain_grid = gain_row.reshape(head_count, HD)
    cubed = inverse * inverse * inverse
    return inverse * gain_grid * upstream - shaped * cubed * jnp.mean(
        shaped * gain_grid * upstream, -1, keepdims=True
    )


def by_clip(grad_rows, clip_ids):
    return jnp.concatenate(
        [
            grad_rows * (clip_ids == clip_no).astype(jnp.bfloat16)[..., None]
            for clip_no in range(CLIPS)
        ],
        -1,
    )


def row_sharded(tokens, w_qkv, gains, cotangent, token_clip, key_live, damp_mask):
    tok_rows = tokens.shape[0]
    width_dev = w_qkv.shape[2]
    rows_dev = w_qkv.shape[1]
    head_count = width_dev // HD
    all_tokens = token_clip.shape[0]
    seq_rank = lax.axis_index("seq")
    score_scale = 1.0 / math.sqrt(HD)
    projected = jnp.einsum(
        "tr,jrc->jtc",
        tokens,
        lax.all_gather(w_qkv, "seq", axis=1, tiled=True),
        preferred_element_type=jnp.float32,
    )
    query_n, query_inv, query_raw = normed(projected[0], gains[0], head_count)
    key_n, key_inv, key_raw = normed(projected[1], gains[1], head_count)
    query_b = query_n.astype(jnp.bfloat16)
    local_kv = jnp.concatenate(
        [
            key_n.astype(jnp.bfloat16).reshape(tok_rows, width_dev),
            projected[2].astype(jnp.bfloat16),
        ],
        1,
    )
    all_kv = lax.all_gather(local_kv, "seq", axis=0, tiled=True)
    keys_all = all_kv[:, :width_dev].reshape(all_tokens, head_count, HD)
    values_all = all_kv[:, width_dev:].reshape(all_tokens, head_count, HD)
    first_row = seq_rank * tok_rows
    clip_here = lax.dynamic_slice_in_dim(token_clip, first_row, tok_rows)
    positions = first_row + jnp.arange(tok_rows, dtype=jnp.int32)
    key_positions = jnp.arange(all_tokens, dtype=jnp.int32)
    allowed = (clip_here[:, None] == token_clip[None, :]) & (
        (key_live[None, :] == 1) | (positions[:, None] == key_positions[None, :])
    )
    scores = (
        jnp.einsum("thd,khd->htk", query_b, keys_all, preferred_element_type=jnp.float32)
        * score_scale
    )
    scores = jnp.where(allowed[None], scores, -1e30)
    peak = jnp.max(scores, -1, keepdims=True)
    expd = jnp.exp(scores - peak)
    probs = expd / jnp.sum(expd, -1, keepdims=True)
    grad_out = cotangent.reshape(tok_rows, head_count, HD)
    grad_p = jnp.einsum("thd,khd->htk", grad_out, values_all, preferred_element_type=jnp.float32)
    row_dot = jnp.sum(probs * grad_p, -1, keepdims=True)
    ds_half = (probs * (grad_p - row_dot)).astype(jnp.bfloat16)
    probs_half = probs.astype(jnp.bfloat16)
    grad_qn = (
        jnp.einsum("htk,khd->thd", ds_half, keys_all, preferred_element_type=jnp.float32)
        * score_scale
    )
    key_part = (
        jnp.einsum("htk,thd->khd", ds_half, query_b, preferred_element_type=jnp.float32)
        * score_scale
    )
    value_part = jnp.einsum(
        "htk,thd->khd", probs_half, grad_out, preferred_element_type=jnp.float32
    )
    key_terms = jnp.concatenate(
        [key_part.reshape(all_tokens, width_dev), value_part.reshape(all_tokens, width_dev)], 1
    )
    summed = lax.psum_scatter(
        key_terms.astype(jnp.bfloat16), "seq", scatter_dimension=0, tiled=True
    ).astype(jnp.float32)
    grad_q = unnorm(grad_qn, query_raw, query_inv, gains[0], head_count)
    grad_k = unnorm(
        summed[:, :width_dev].reshape(tok_rows, head_count, HD),
        key_raw,
        key_inv,
        gains[1],
        head_count,
    )
    grad_proj = jnp.concatenate(
        [
            grad_q.reshape(tok_rows, width_dev),
            grad_k.reshape(tok_rows, width_dev),
            summed[:, width_dev:],
        ],
        1,
    ).astype(jnp.bfloat16)
    masked = by_clip(grad_proj, clip_here)
    per_clip = lax.psum_scatter(
        lax.dot_general(
            tokens, masked, (((0,), (0,)), ((), ())), preferred_element_type=jnp.float32
        ).astype(jnp.bfloat16),
        "seq",
        scatter_dimension=0,
        tiled=True,
    ).astype(jnp.float32)
    fisher = jnp.sum(jnp.square(per_clip.reshape(rows_dev, CLIPS, 3, width_dev)), 1)
    fisher = jnp.transpose(fisher, (1, 0, 2))
    fisher_sum = lax.psum(jnp.sum(fisher), AXES)
    fisher_mean = fisher_sum / (3 * D * HEADS * HD)
    fisher_ratio = fisher / (fisher_mean + EPS)
    dampened = (
        w_qkv.astype(jnp.float32) / (1.0 + damp_mask.astype(jnp.float32)[None] * fisher_ratio)
    ).astype(jnp.bfloat16)
    return (fisher_ratio, dampened)


def token_copies(layout, arrays, place, bases, first, target, block_row, sem):
    copies = []
    for n, (array, row, block, base, offset, count) in enumerate(layout):
        start = block_row(block - first) + place[bases + base] + offset
        copies.append(
            pltpu.make_async_copy(
                arrays[array].at[pl.ds(row, count)],
                target.at[pl.ds(pl.multiple_of(start, 16), count)],
                sem.at[n],
            )
        )
    return copies


def project_kernel(nb, na, tb, rows, quarter, layout, bases, first, nb_all, with_cot, place, *refs):
    chunks = refs[:na]
    pieces = refs[na : na + quarter]
    outs = refs[na + quarter : -6]
    xs, ws, cs, xsem, wsem, csem = refs[-6:]
    copies = []
    for k in range(quarter):
        start = pl.multiple_of(place[nb_all + k] * rows, rows)
        for j in range(3):
            copies.append(
                pltpu.make_async_copy(
                    pieces[k].at[pl.ds(j * rows, rows)],
                    ws.at[pl.ds(start, rows), pl.ds(j * HD, HD)],
                    wsem.at[k, j],
                )
            )
        if with_cot:
            copies.append(
                pltpu.make_async_copy(
                    pieces[k].at[pl.ds(3 * rows, tb)], cs.at[pl.ds(k * tb, tb)], csem.at[k]
                )
            )
    xcopies = token_copies(layout, chunks, place, bases, first, xs, lambda b: b * tb, xsem)
    for copy in copies + xcopies:
        copy.start()
    for copy in copies:
        copy.wait()
    if with_cot:
        outs[1][...] = cs[...]
    for copy in xcopies:
        copy.wait()
    part = jnp.dot(xs[...], ws[...], preferred_element_type=jnp.float32)
    outs[0][...] = part.astype(jnp.bfloat16)


def project(arrays, layout, first, nb, nb_all, pieces, place, bases, tb, with_cot):
    quarter = len(pieces)
    used = sorted({entry[0] for entry in layout})
    layout = tuple((used.index(entry[0]), *entry[1:]) for entry in layout)
    arrays = [arrays[i] for i in used]
    half = arrays[0].shape[1]
    rows = (pieces[0].shape[0] - tb) // 3
    vmem = pl.BlockSpec(memory_space=pltpu.VMEM)
    shapes = [jax.ShapeDtypeStruct((nb * tb, 3 * HD), jnp.bfloat16)]
    if with_cot:
        shapes.append(jax.ShapeDtypeStruct((quarter * tb, HD), jnp.bfloat16))
    return pl.pallas_call(
        functools.partial(
            project_kernel, nb, len(arrays), tb, rows, quarter, layout, bases, first, nb_all, with_cot
        ),
        out_shape=shapes,
        in_specs=[pl.BlockSpec(memory_space=pltpu.SMEM)]
        + [pl.BlockSpec(memory_space=pl.ANY)] * (len(arrays) + quarter),
        out_specs=[vmem] * len(shapes),
        scratch_shapes=[
            pltpu.VMEM((nb * tb, half), jnp.bfloat16),
            pltpu.VMEM((half, 3 * HD), jnp.bfloat16),
            pltpu.VMEM((quarter * tb, HD), jnp.bfloat16),
            pltpu.SemaphoreType.DMA((len(layout),)),
            pltpu.SemaphoreType.DMA((quarter, 3)),
            pltpu.SemaphoreType.DMA((quarter,)),
        ],
        compiler_params=pltpu.CompilerParams(vmem_limit_bytes=VMEM_BYTES),
        cost_estimate=pl.CostEstimate(flops=8800000000, bytes_accessed=28800000, transcendentals=0),
        name="project",
    )(place, *arrays, *pieces)


def cover(total, unit):
    count = max(1, total // unit)
    return (unit,) * (count - 1) + (total - unit * (count - 1),)


def head_kernel(nb, nc, tb, rows, quarter, parts, layout, bases, spans, place, windows, *refs):
    chunks = refs[:nc]
    cots = refs[nc : nc + 2]
    ends = nc + 2 + 2 * len(parts)
    projections = refs[nc + 2 : ends]
    gain, clip_row, key_row, clips = refs[ends : ends + 4]
    fisher_out = refs[ends + 4 : ends + 4 + quarter]
    sum_out = refs[ends + 4 + quarter]
    (do, q_raw_t, k_raw, qn, kn, vb, qn_t, kn_t, do_t, key_code, es, dps, dk, dv) = refs[
        ends + 5 + quarter : -5
    ]
    dproj_t, xs, squares, xsem, csem = refs[-5:]
    scale = 1.0 / math.sqrt(HD)
    cot_copies = []
    for k in range(quarter):
        for side in range(2):
            src = cots[side].at[pl.ds(k * tb, tb)]
            block = place[nb + quarter * (1 + side) + k]
            cot_copies.append(
                pltpu.make_async_copy(
                    src, do.at[pl.ds(pl.multiple_of(block * tb, tb), tb)], csem.at[side, k]
                )
            )
    xcopies = token_copies(
        layout, chunks, place, bases, 0, xs, lambda b: place[b] * tb, xsem
    )
    for copy in cot_copies + xcopies:
        copy.start()
    q_gain_t = jnp.concatenate([jnp.broadcast_to(gain[0:1, :], (HD, HD)).T] * (tb // HD), 1)

    first_block = 0
    for part, count in enumerate(parts):

        def normalise(b, carry, first_block=first_block, part=part):
            source = pl.ds(pl.multiple_of(b * tb, tb), tb)
            block = place[first_block + b]
            here = pl.ds(pl.multiple_of(block * tb, tb), tb)
            mine, other = projections[2 * part : 2 * part + 2]
            total = mine[source, :].astype(jnp.float32) + other[source, :].astype(jnp.float32)
            raw = total[:, :HD]
            inv = lax.rsqrt(jnp.mean(raw * raw, -1, keepdims=True) + EPS)
            qn[here, :] = (raw * inv * gain[0:1, :]).astype(jnp.bfloat16)
            raw_t = raw.T
            inv = lax.rsqrt(jnp.mean(raw_t * raw_t, 0, keepdims=True) + EPS)
            q_raw_t[block] = raw_t
            qn_t[block] = (raw_t * inv * q_gain_t).astype(jnp.bfloat16)
            raw = total[:, HD : 2 * HD]
            k_raw[here, :] = raw
            inv = lax.rsqrt(jnp.mean(raw * raw, -1, keepdims=True) + EPS)
            value = raw * inv * gain[1:2, :]
            kn[here, :] = value.astype(jnp.bfloat16)
            value_t = value.T.astype(jnp.bfloat16)
            for u in range(tb // HD):
                kn_t[block * (tb // HD) + u] = value_t[:, u * HD : (u + 1) * HD]
            vb[here, :] = total[:, 2 * HD :].astype(jnp.bfloat16)
            key_code[here, :] = jnp.broadcast_to(key_row[block], (HD, tb)).T
            return carry

        lax.fori_loop(0, count, normalise, 0)
        first_block += count
    for copy in cot_copies:
        copy.wait()

    def prepare(b, carry):
        here = pl.ds(pl.multiple_of(b * tb, tb), tb)
        do_t[b] = do[here, :].astype(jnp.float32).T.astype(jnp.bfloat16)
        dk[here, :] = jnp.zeros((tb, HD), jnp.float32)
        dv[here, :] = jnp.zeros((tb, HD), jnp.float32)
        return carry

    lax.fori_loop(0, nb, prepare, 0)

    def backward_norm(upstream, raw, weight, axis):
        inv = lax.rsqrt(jnp.mean(raw * raw, axis, keepdims=True) + EPS)
        weighted = weight * upstream
        cubed = inv * inv * inv
        return inv * weighted - raw * (cubed * jnp.mean(raw * weighted, axis, keepdims=True))

    def tile(start, length):
        here = pl.ds(pl.multiple_of(start, HD), length)
        offset = lax.broadcasted_iota(jnp.int32, (length, tb), 0) - lax.broadcasted_iota(
            jnp.int32, (length, tb), 1
        )
        return here, offset

    def forward(i, start, at, length, sums):
        here, offset = tile(start + at, length)
        s = jnp.dot(kn[here, :], qn_t[i], preferred_element_type=jnp.float32)
        codes = jnp.concatenate([key_code[here, :]] * (tb // HD), 1)
        allowed = (codes == clip_row[i]) | (offset == i * tb - start - at)
        e = jnp.where(allowed, jnp.exp2(s * (scale * math.log2(math.e))), 0.0)
        dp = jnp.dot(vb[here, :], do_t[i], preferred_element_type=jnp.float32)
        es[at : at + length, :] = e
        dps[at : at + length, :] = dp
        return (
            sums[0] + jnp.sum(e.reshape(length // 8, 8, tb), 0),
            sums[1] + jnp.sum((e * dp).reshape(length // 8, 8, tb), 0),
        )

    def finish_sums(sums):
        inv_l = 1.0 / jnp.sum(sums[0], 0, keepdims=True)
        return inv_l, jnp.sum(sums[1], 0, keepdims=True) * inv_l

    def backward(i, start, at, length, inv_l, row_dot, dq_t):
        here, _ = tile(start + at, length)
        rows_q = columns(i)
        p = es[at : at + length, :] * inv_l
        ds = (p * (dps[at : at + length, :] - row_dot)).astype(jnp.bfloat16)
        dv[here, :] += jnp.dot(
            p.astype(jnp.bfloat16), do[rows_q, :], preferred_element_type=jnp.float32
        )
        dk[here, :] += jnp.dot(ds, qn[rows_q, :], preferred_element_type=jnp.float32)
        first = (start + at) // HD
        for u in range(0, length, tb):
            keys_t = jnp.concatenate(
                [kn_t[first + (u + v) // HD] for v in range(0, min(tb, length - u), HD)], 1
            )
            dq_t += jnp.dot(keys_t, ds[u : u + tb], preferred_element_type=jnp.float32)
        return dq_t

    def columns(i):
        return pl.ds(pl.multiple_of(i * tb, tb), tb)

    def store_dq(i, dq_t):
        dproj_t[:HD, columns(i)] = backward_norm(dq_t * scale, q_raw_t[i], q_gain_t, 0).astype(
            jnp.bfloat16
        )

    zero = jnp.zeros((8, tb), jnp.float32)

    def query_block(i, start, lengths):
        sums = (zero, zero)
        at = 0
        for length in lengths:
            sums = forward(i, start, at, length, sums)
            at += length
        inv_l, row_dot = finish_sums(sums)
        dq_t = jnp.zeros((HD, tb), jnp.float32)
        at = 0
        for length in lengths:
            dq_t = backward(i, start, at, length, inv_l, row_dot, dq_t)
            at += length
        store_dq(i, dq_t)

    def queries(i, carry):
        inside = (place[nb + 3 * quarter + i] == windows[len(spans)]) & (
            place[2 * nb + 3 * quarter + i] == windows[len(spans)]
        )

        @pl.when(inside)
        def _():
            query_block(i, windows[0], cover(spans[0], 2 * tb))

        @pl.when(jnp.logical_not(inside))
        def _():
            query_block(i, 0, cover(nb * tb, 2 * tb))

        return carry

    lax.fori_loop(0, nb, queries, 0)

    def keys(b, carry):
        here = columns(b)
        value = backward_norm(dk[here, :] * scale, k_raw[here, :], gain[1:2, :], -1)
        dproj_t[HD : 2 * HD, here] = value.T.astype(jnp.bfloat16)
        dproj_t[2 * HD :, here] = dv[here, :].T.astype(jnp.bfloat16)
        return carry

    lax.fori_loop(0, nb, keys, 0)

    for copy in xcopies:
        copy.wait()
    for i, length in enumerate(spans):
        span = pl.ds(pl.multiple_of(windows[i], HD), length)
        mask = (clips[:, span] == windows[len(spans) + i]).astype(jnp.float32)
        part = jnp.dot(
            dproj_t[:, span] * mask.astype(jnp.bfloat16),
            xs[span, :],
            preferred_element_type=jnp.float32,
        )
        squares[...] = part * part if i == 0 else squares[...] + part * part
    running = jnp.zeros((3 * HD, rows), jnp.float32)
    for k in range(quarter):
        lanes = pl.ds(pl.multiple_of(place[nb + k] * rows, rows), rows)
        piece = squares[:, lanes]
        running += piece
        for j in range(3):
            fisher_out[k][j * rows : (j + 1) * rows, :] = (
                piece[j * HD : (j + 1) * HD, :].T.astype(jnp.bfloat16)
            )
    sum_out[...] = jnp.full((8, HD), jnp.sum(running), jnp.float32)


def finish_kernel(quarter, rows, shift, total, w, mask, *refs):
    pieces = refs[:quarter]
    ratio_out, damp_out, w_in, mask_in, ratio_buf, damp_buf, in_sem, out_sem = refs[quarter:]
    loads, stores = [], []
    for k in range(quarter):
        lanes = pl.ds(pl.multiple_of(lax.rem(shift[0] + k, quarter) * HD, HD), HD)
        loads.append(
            (
                pltpu.make_async_copy(w.at[:, :, lanes], w_in.at[k], in_sem.at[0, k]),
                pltpu.make_async_copy(mask.at[:, lanes], mask_in.at[k], in_sem.at[1, k]),
            )
        )
        stores.append(
            (
                pltpu.make_async_copy(ratio_buf.at[k], ratio_out.at[:, :, lanes], out_sem.at[0, k]),
                pltpu.make_async_copy(damp_buf.at[k], damp_out.at[:, :, lanes], out_sem.at[1, k]),
            )
        )
    for pair in loads:
        for copy in pair:
            copy.start()
    mean = total[0, 0] * (1.0 / (3 * D * HEADS * HD))
    factor = 1.0 / jnp.full((1, HD), mean + EPS, jnp.float32)
    for k in range(quarter):
        for copy in loads[k]:
            copy.wait()
        damp = mask_in[k].astype(jnp.float32)
        for j in range(3):
            ratio = pieces[k][j * rows : (j + 1) * rows, :].astype(jnp.float32) * factor
            ratio_buf[k, j] = ratio
            damp_buf[k, j] = (w_in[k, j].astype(jnp.float32) / (1.0 + damp * ratio)).astype(
                jnp.bfloat16
            )
        for copy in stores[k]:
            copy.start()
    for pair in stores:
        for copy in pair:
            copy.wait()


def chip_per_head(tokens, w_qkv, gains, cotangent, token_clip, key_live, damp_mask, *, ns, nh):
    tb, width = tokens.shape
    rows, cols = w_qkv.shape[1:]
    quarter = cols // HD
    half = width // 2
    all_tokens = token_clip.shape[0]
    s = lax.axis_index("seq")
    h = lax.axis_index("head")
    core = h % 2
    vmem = pl.BlockSpec(memory_space=pltpu.VMEM)
    smem = pl.BlockSpec(memory_space=pltpu.SMEM)
    hbm = pl.BlockSpec(memory_space=pl.ANY)

    def index(si, hi):
        return si * nh + hi

    swap = [(index(a, b), index(a, b ^ 1)) for a in range(ns) for b in range(nh)]
    out_perms = []
    for k in range(quarter):
        out_perms.append(
            [
                (index(a, b), index((b % 2) * quarter + (k + a) % quarter, b - b % 2 + a // quarter))
                for a in range(ns)
                for b in range(nh)
            ]
        )
    back_perms = [[(b, a) for a, b in perm] for perm in out_perms]

    gains_other = lax.ppermute(gains, AXES, swap)
    outgoing = []
    for k in range(quarter):
        col = ((k + s) % quarter) * HD
        outgoing.append(
            jnp.concatenate(
                [
                    lax.dynamic_slice_in_dim(w_qkv, col, HD, 2).reshape(3 * rows, HD),
                    lax.dynamic_slice_in_dim(cotangent, col, HD, 1),
                ],
                0,
            )
        )
    ring = list(range(0, ns, 2)) + list(range(1, ns, 2))[::-1]
    forth = [(ring[i], ring[(i + 1) % ns]) for i in range(ns)]
    back = [(b, a) for a, b in forth]
    position = [ring.index(i) for i in range(ns)]
    mine = lax.dynamic_slice_in_dim(tokens, core * half, half, 1)
    share = 80
    carried = tb - share
    side = h // 2 % 2
    across = [(i, i ^ 2) for i in range(nh)]
    missing = side * (carried - share)
    pieces = {}
    plan = {2: (0, 1), 3: (2, 3)}

    def tie(step, *arrays):
        for k in plan.get(step, ()):
            pieces[k] = lax.ppermute(outgoing[k], AXES, out_perms[k])
        out = lax.optimization_barrier((*arrays, *[pieces[k] for k in plan.get(step, ())]))
        for k, piece in zip(plan.get(step, ()), out[len(arrays) :]):
            pieces[k] = piece
        return out[: len(arrays)]

    arrays, layout, steps = [mine], [(0, 0, 0, 0, 0, tb)], [0]
    ahead = behind = lax.dynamic_slice_in_dim(mine, side * share, carried, 0)
    for step in range(1, ns // 2):
        if step > 1:
            ahead, behind = tie(step, ahead, behind)
        ahead = lax.ppermute(ahead, "seq", forth)
        behind = lax.ppermute(behind, "seq", back)
        both = jnp.concatenate(
            [lax.dynamic_slice_in_dim(a, missing, share, 0) for a in (ahead, behind)], 0
        )
        n, block = len(arrays), len(steps)
        arrays += [ahead, behind, lax.ppermute(both, "head", across)]
        layout += [
            (n, 0, block, 1, 0, carried),
            (n + 1, 0, block + 1, 1, 0, carried),
            (n + 2, 0, block, 2, 0, share),
            (n + 2, share, block + 1, 2, 0, share),
        ]
        steps += [-step, step]
    cut = carried - share
    ahead = lax.ppermute(ahead[:cut], "seq", forth)
    behind = lax.ppermute(behind[cut:], "seq", back)
    both = jnp.where(side == 0, ahead[:share], behind)
    n, block = len(arrays), len(steps)
    arrays += [ahead, behind, lax.ppermute(both, "head", across)]
    layout += [
        (n, 0, block, 1, 0, cut),
        (n + 1, 0, block, 1, cut, share),
        (n + 2, 0, block, 2, 0, share),
    ]
    steps.append(ns // 2)
    pieces = [pieces[k] for k in range(quarter)]
    blocks = token_clip.reshape(ns, tb)
    edges = (blocks[:, 0], blocks[:, -1])
    order = jnp.array([[ring[(position[i] + d) % ns] for d in steps] for i in range(ns)], jnp.int32)
    ks = jnp.arange(quarter, dtype=jnp.int32)
    row_block = ((s - ks) % quarter).astype(jnp.int32)
    place = jnp.concatenate(
        [
            lax.dynamic_index_in_dim(order, s, 0, False),
            row_block,
            row_block + core * quarter,
            row_block + (1 - core) * quarter,
            *edges,
            jnp.stack([0 * side, side * share, (1 - side) * carried]),
        ]
    ).astype(jnp.int32)

    params = pltpu.CompilerParams(vmem_limit_bytes=VMEM_BYTES)
    bf16, f32 = jnp.bfloat16, jnp.float32
    own_gain = (s // quarter) == core
    gain = lax.dynamic_slice_in_dim(
        jnp.where(own_gain, gains, gains_other), (s % quarter) * HD, HD, 1
    )
    clip_row = token_clip.reshape(ns, 1, tb)
    key_row = jnp.where(key_live == 1, token_clip, -1).reshape(ns, 1, tb)
    clip_ids = jnp.arange(CLIPS, dtype=jnp.int32)
    starts = jnp.sum(token_clip[None] < clip_ids[:, None], 1, dtype=jnp.int32)
    sizes = jnp.sum(token_clip[None] == clip_ids[:, None], 1, dtype=jnp.int32)
    longest = jnp.argmax(sizes).astype(jnp.int32)
    ordered = jnp.stack([longest] + [(longest + i) % CLIPS for i in range(1, CLIPS)])
    spans = (3 * all_tokens // 4 + HD,) + (all_tokens // 4 + HD,) * (CLIPS - 1)
    windows = jnp.minimum(starts[ordered] // HD * HD, all_tokens - jnp.array(spans, jnp.int32))
    windows = jnp.concatenate([windows, ordered]).astype(jnp.int32)
    place, windows, gain, clip_row, key_row, *pieces = lax.optimization_barrier(
        (place, windows, gain, clip_row, key_row, *pieces)
    )
    parts = (ns - 3, 3)
    bases = 3 * ns + 3 * quarter
    projections = []
    first = 0
    for part, count in enumerate(parts):
        entries = [entry for entry in layout if first <= entry[2] < first + count]
        partial, *cot = project(
            arrays, entries, first, count, ns, pieces, place, bases, tb, part == 0
        )
        projections += [partial, lax.ppermute(partial, AXES, swap)]
        first += count
        if part == 0:
            cot_mine = cot[0]
            cot_other = lax.ppermute(cot_mine, AXES, swap)
    *fisher, part_sum = pl.pallas_call(
        functools.partial(
            head_kernel, ns, len(arrays), tb, rows, quarter, parts, tuple(layout), bases, spans
        ),
        out_shape=(
            *[jax.ShapeDtypeStruct((3 * rows, HD), bf16)] * quarter,
            jax.ShapeDtypeStruct((8, HD), f32),
        ),
        in_specs=[smem, smem] + [hbm] * (len(arrays) + 2) + [vmem] * (len(projections) + 4),
        out_specs=[vmem] * (quarter + 1),
        scratch_shapes=[
            pltpu.VMEM((all_tokens, HD), bf16),
            pltpu.VMEM((ns, HD, tb), f32),
            pltpu.VMEM((all_tokens, HD), f32),
            pltpu.VMEM((all_tokens, HD), bf16),
            pltpu.VMEM((all_tokens, HD), bf16),
            pltpu.VMEM((all_tokens, HD), bf16),
            pltpu.VMEM((ns, HD, tb), bf16),
            pltpu.VMEM((all_tokens // HD, HD, HD), bf16),
            pltpu.VMEM((ns, HD, tb), bf16),
            pltpu.VMEM((all_tokens, HD), jnp.int32),
            pltpu.VMEM((all_tokens, tb), f32),
            pltpu.VMEM((all_tokens, tb), f32),
            pltpu.VMEM((all_tokens, HD), f32),
            pltpu.VMEM((all_tokens, HD), f32),
            pltpu.VMEM((3 * HD, all_tokens), bf16),
            pltpu.VMEM((all_tokens, half), bf16),
            pltpu.VMEM((3 * HD, half), f32),
            pltpu.SemaphoreType.DMA((len(layout),)),
            pltpu.SemaphoreType.DMA((2, quarter)),
        ],
        compiler_params=params,
        cost_estimate=pl.CostEstimate(flops=34100000000, bytes_accessed=111600000, transcendentals=0),
        name="head",
    )(
        place,
        windows,
        *arrays,
        cot_mine,
        cot_other,
        *projections,
        gain,
        clip_row,
        key_row,
        token_clip[None],
    )

    returned = [lax.ppermute(fisher[k], AXES, back_perms[k]) for k in range(quarter)]
    total = part_sum[:1]
    bit = 1
    while bit < nh:
        total = total + lax.ppermute(total, "head", [(i, i ^ bit) for i in range(nh)])
        bit *= 2
    bit = 1
    while bit < ns:
        total = total + lax.ppermute(total, "seq", [(i, i ^ bit) for i in range(ns)])
        bit *= 2
    shift = (s % quarter).astype(jnp.int32).reshape(1)
    hbm_only = pl.BlockSpec(memory_space=pltpu.HBM)
    return pl.pallas_call(
        functools.partial(finish_kernel, quarter, rows),
        out_shape=(
            jax.ShapeDtypeStruct((3, rows, cols), f32),
            jax.ShapeDtypeStruct((3, rows, cols), bf16),
        ),
        in_specs=[smem, smem, hbm_only, hbm_only] + [vmem] * quarter,
        out_specs=[hbm_only] * 2,
        scratch_shapes=[
            pltpu.VMEM((quarter, 3, rows, HD), bf16),
            pltpu.VMEM((quarter, rows, HD), jnp.int32),
            pltpu.VMEM((quarter, 3, rows, HD), f32),
            pltpu.VMEM((quarter, 3, rows, HD), bf16),
            pltpu.SemaphoreType.DMA((2, quarter)),
            pltpu.SemaphoreType.DMA((2, quarter)),
        ],
        compiler_params=params,
        cost_estimate=pl.CostEstimate(flops=5500000000, bytes_accessed=18000000, transcendentals=0),
        name="finish",
    )(shift, total, w_qkv, damp_mask, *returned)


def solution(mesh):
    ns, nh = mesh.shape["seq"], mesh.shape["head"]

    def on_device(*args):
        if ns == 2 * (args[1].shape[2] // HD) and ns & (ns - 1) == 0 and nh % 4 == 0 and args[4].shape[0] % (4 * HD) == 0:
            return chip_per_head(*args, ns=ns, nh=nh)
        return row_sharded(*args)

    return jax.shard_map(
        on_device,
        mesh=mesh,
        in_specs=(
            P("seq", None),
            P(None, "seq", "head"),
            P(None, "head"),
            P("seq", "head"),
            P(),
            P(),
            P("seq", "head"),
        ),
        out_specs=(P(None, "seq", "head"), P(None, "seq", "head")),
        check_vma=False,
    )
```
